256 devices in a mesh: mem: 64 (over z, x, y_hi), grp: 4 (over y_lo, core).
Axes of the slice: x: 4, y: 4 (y_hi: 2, y_lo: 2; y = y_hi * 2 + y_lo), z: 8, core: 2. Of those that a mesh axis runs over, the one named last changes fastest.
Arguments:
- fields: bfloat16 [4, 1024, 4, 64, 256], P('grp', 'mem'), may hold values from -6 to 6
- centres: bfloat16 [4, 64, 1024, 1024], P('grp', 'mem'), may hold values from -0.03125 to 1
- sides: int32 [4, 64, 4, 2], P('grp', 'mem'), may hold values from 0 to 1
- quarters: int32 [4, 64, 4, 2], P('grp', 'mem'), may hold values from 0 to 4
Outputs:
- analysis: bfloat16 [4, 1024, 4, 64, 256], P('grp', 'mem')
The draws below stay inside these ranges and needn't reach their ends.
All inputs are finite; a program needn't handle non-finite values.
Results may differ from the reference program's by a relative error of at most 0.006.
Values may be sent and summed in bfloat16 or wider, within the bound.
No kernel may reach another device: no remote copies, remote signals or barrier semaphores. Data moves between devices by JAX's collectives and lax.ppermute only.
A program may use at most 128 MiB of HBM per device.

```python
import jax
import jax.numpy as jnp
from jax import lax

K = 1024
SUBS = 4
COLP = 256
LEVELS = 4
PR = 4
PC = 64


def draw_centres(key, part):
    key = jax.random.fold_in(key, 7)
    raw = jax.random.uniform(key, (PR, PC, K, K), jnp.float32)
    eye_mask = jnp.eye(K, dtype=jnp.float32)
    low = jnp.min(jnp.where(eye_mask > 0.5, 1.0, raw))
    high = jnp.max(jnp.where(eye_mask > 0.5, 0.0, raw))
    spread = 1.0 / jnp.sqrt(jnp.float32(K))
    off_diag = spread * (2.0 * (raw - low) / (high - low) - 1.0)
    return (eye_mask + off_diag * (1.0 - eye_mask)).astype(jnp.bfloat16)


def touch_ends(array, rng, least, high):
    extent = array.shape
    spot = [jax.random.randint(jax.random.fold_in(rng, axis), (), 0, extent[axis]) for axis in range(len(extent))]
    array = array.at[tuple(spot)].set(least)
    longest = extent.index(max(extent))
    spot[longest] = (spot[longest] + 1) % extent[longest]
    return array.at[tuple(spot)].set(high)


def levels(rng, extent, pieces, least, high):
    loudness, own = 1.0, jax.random.fold_in(rng, 6)
    for dim, blocks in pieces:
        draws = jnp.exp(jax.random.uniform(jax.random.fold_in(own, dim), (blocks,), jnp.float32, least / len(pieces), high / len(pieces)))
        loudness = loudness * jnp.repeat(draws, extent[dim] // blocks).reshape([-1 if axis == dim else 1 for axis in range(len(extent))])
    return loudness


def centred(own_key, shape, scale, bound, shards=(), kind=jnp.bfloat16):
    gain = levels(own_key, shape, shards, -0.22, 0.18) if shards else 1.0
    values = jax.random.normal(own_key, shape, jnp.float32) * scale * gain
    return jnp.minimum(jnp.maximum(values, -bound), bound).astype(kind)


def setup_inputs(seed: int = 0) -> dict:
    arg_keys = jax.random.split(jax.random.key(seed), 5)
    fields = centred(arg_keys[0], (LEVELS, K, PR, PC, COLP), 1.0, 6.0, ((0, 4), (1, 64)))
    centres = draw_centres(jax.random.fold_in(arg_keys[4], 71), 0)
    sides = touch_ends(jax.random.randint(arg_keys[2], (PR, PC, SUBS, 2), 0, 2), jax.random.fold_in(arg_keys[2], 1), 0, 1).astype(jnp.int32)
    quarters = touch_ends(jax.random.randint(arg_keys[3], (PR, PC, SUBS, 2), 0, 5), jax.random.fold_in(arg_keys[3], 1), 0, 4).astype(jnp.int32)
    return dict(fields=fields, centres=centres, sides=sides, quarters=quarters)


def reference(fields, centres, sides, quarters):
    patch_fields = jnp.transpose(fields, (2, 3, 0, 1, 4)).reshape(PR * PC, LEVELS, K, COLP)

    def one_patch(patch_id):
        row_id = patch_id // PC
        col_id = patch_id % PC
        side_row = sides[row_id, col_id, :, 0]
        side_col = sides[row_id, col_id, :, 1]
        row_next = (row_id + 2 * side_row - 1) % PR
        col_next = (col_id + 2 * side_col - 1) % PC
        frac_row = quarters[row_id, col_id, :, 0].astype(jnp.float32) / 4.0
        frac_col = quarters[row_id, col_id, :, 1].astype(jnp.float32) / 4.0
        row_same = jnp.zeros_like(side_row) + row_id
        col_same = jnp.zeros_like(side_col) + col_id
        own_mat = centres[row_same, col_same].astype(jnp.float32)
        row_mat = centres[row_next, col_same].astype(jnp.float32)
        col_mat = centres[row_same, col_next].astype(jnp.float32)
        diag_mat = centres[row_next, col_next].astype(jnp.float32)
        blend = (((1.0 - frac_row) * (1.0 - frac_col))[:, None, None] * own_mat
                 + (frac_row * (1.0 - frac_col))[:, None, None] * row_mat
                 + ((1.0 - frac_row) * frac_col)[:, None, None] * col_mat
                 + (frac_row * frac_col)[:, None, None] * diag_mat)
        block_field = patch_fields[patch_id].reshape(LEVELS, K, SUBS, 64).astype(jnp.float32)
        analysed = jnp.einsum('lksc,skj->ljsc', block_field, blend, precision=lax.Precision.HIGHEST)
        return analysed.reshape(LEVELS, K, COLP).astype(jnp.bfloat16)

    result = lax.map(one_patch, jnp.arange(PR * PC, dtype=jnp.int32))
    return jnp.transpose(result.reshape(PR, PC, LEVELS, K, COLP), (2, 3, 0, 1, 4))
```

```python
import functools

import jax
import jax.numpy as jnp
from jax import lax
from jax.experimental import pallas as pl
from jax.experimental.pallas import tpu as pltpu
from jax.sharding import PartitionSpec as P

AX = ("mem", "grp")
MEM = 64
GRP = 4
K = 1024
JQ = 256


def flat_perm(move):
    pairs = []
    for mem in range(MEM):
        for grp in range(GRP):
            to_mem, to_grp = move(mem, grp)
            pairs.append((mem * GRP + grp, (to_mem % MEM) * GRP + to_grp))
    return pairs


CORE = flat_perm(lambda m, g: (m, g ^ 1))
PAL = flat_perm(lambda m, g: (m, g ^ 2))
CROSS = flat_perm(lambda m, g: (m ^ 1, g ^ 2))
SIDE = flat_perm(lambda m, g: (m + 2 if m % 2 else m - 2, g))


def split_kernel(where_ref, centre_ref, *outs):
    grp = where_ref[0]
    parity = where_ref[1]
    row = lax.broadcasted_iota(jnp.int32, (JQ, K), 0)
    col = lax.broadcasted_iota(jnp.int32, (JQ, K), 1)
    base = (row // 4) * 16 + row % 4
    for rho in range(GRP):
        quarter = lax.bitwise_xor(lax.bitwise_xor(grp, rho), 2 * parity)
        pick = jnp.where(col == base + 4 * quarter, 1.0, 0.0).astype(jnp.bfloat16)
        outs[rho][...] = lax.dot_general(
            pick,
            centre_ref[...],
            (((1,), (1,)), ((), ())),
            preferred_element_type=jnp.float32,
        ).astype(jnp.bfloat16)


def split_centres(where, centre):
    return pl.pallas_call(
        split_kernel,
        out_shape=[jax.ShapeDtypeStruct((JQ, K), jnp.bfloat16)] * GRP,
        in_specs=[
            pl.BlockSpec(memory_space=pltpu.SMEM),
            pl.BlockSpec(memory_space=pltpu.VMEM),
        ],
        out_specs=[pl.BlockSpec(memory_space=pltpu.VMEM)] * GRP,
        compiler_params=pltpu.CompilerParams(vmem_limit_bytes=40 * 1024 * 1024),
        cost_estimate=pl.CostEstimate(flops=2 * K * K * K, bytes_accessed=4 * K * K, transcendentals=0),
    )(where, centre)


def apply_kernel(where_ref, params_ref, *refs):
    pieces = refs[:12]
    fields = refs[12:16]
    out_ref = refs[16]
    table, blend, sems = refs[17:]
    row = pl.program_id(0)
    grp = where_ref[0]
    parity = where_ref[1]

    @pl.when(row == 0)
    def _():
        copies = [
            pltpu.make_async_copy(pieces[i], table.at[i], sems.at[i]) for i in range(12)
        ]
        for copy in copies:
            copy.start()
        for copy in copies:
            copy.wait()

    lane = lax.broadcasted_iota(jnp.int32, (JQ, 128), 1)
    for pair in range(2):
        for half in range(2):
            sub = 2 * pair + half
            side_row = params_ref[row, sub, 0]
            side_col = params_ref[row, sub, 1]
            a = params_ref[row, sub, 2].astype(jnp.float32) * 0.25
            b = params_ref[row, sub, 3].astype(jnp.float32) * 0.25
            row2 = lax.bitwise_and(row + 2 * side_row - 1, 3)
            base2 = jnp.where(side_col == parity, 0, 4)
            i_own = 8 + lax.bitwise_xor(lax.bitwise_xor(row, grp), 2)
            i_row = 8 + lax.bitwise_xor(lax.bitwise_xor(row2, grp), 2)
            i_col = base2 + lax.bitwise_xor(row, grp)
            i_diag = base2 + lax.bitwise_xor(row2, grp)
            w_own = (1.0 - a) * (1.0 - b)
            w_row = a * (1.0 - b)
            w_col = (1.0 - a) * b
            w_diag = a * b

            @pl.loop(0, JQ // 32)
            def _(step):
                at = pl.ds(pl.multiple_of(step * 32, 32), 32)
                mixed = w_own * table[i_own, at, :].astype(jnp.float32)
                mixed = mixed + w_row * table[i_row, at, :].astype(jnp.float32)
                mixed = mixed + w_col * table[i_col, at, :].astype(jnp.float32)
                mixed = mixed + w_diag * table[i_diag, at, :].astype(jnp.float32)
                to = pl.ds(pl.multiple_of(half * JQ + step * 32, 32), 32)
                blend[to, :] = mixed.astype(jnp.bfloat16)

        for two in range(2):
            right = jnp.concatenate(
                [
                    fields[2 * two + i][:, 0, :, pair * 128 : pair * 128 + 128].reshape(K, 128)
                    for i in range(2)
                ],
                axis=1,
            )
            product = jnp.dot(blend[...], right, preferred_element_type=jnp.float32)
            for i in range(2):
                rho = 2 * two + i
                level = lax.bitwise_xor(grp, rho)
                low = product[:JQ, i * 128 : i * 128 + 128]
                high = product[JQ:, i * 128 : i * 128 + 128]
                out_ref[level, 0, :, pair * 128 : pair * 128 + 128] = jnp.where(
                    lane < 64, low, high
                ).astype(jnp.bfloat16)


def apply_transforms(where, params, pieces, fields):
    return pl.pallas_call(
        apply_kernel,
        grid=(4,),
        out_shape=jax.ShapeDtypeStruct((4, 4, JQ, 256), jnp.bfloat16),
        in_specs=[
            pl.BlockSpec(memory_space=pltpu.SMEM),
            pl.BlockSpec(memory_space=pltpu.SMEM),
        ]
        + [pl.BlockSpec(memory_space=pl.ANY)] * 12
        + [pl.BlockSpec((MEM, 1, 16, 256), lambda r: (0, r, 0, 0))] * 4,
        out_specs=pl.BlockSpec((4, 1, JQ, 256), lambda r: (0, r, 0, 0)),
        scratch_shapes=[
            pltpu.VMEM((12, JQ, K), jnp.bfloat16),
            pltpu.VMEM((2 * JQ, K), jnp.bfloat16),
            pltpu.SemaphoreType.DMA((12,)),
        ],
        compiler_params=pltpu.CompilerParams(vmem_limit_bytes=40 * 1024 * 1024),
        cost_estimate=pl.CostEstimate(
            flops=4 * K * K * K, bytes_accessed=16 * K * K, transcendentals=0
        ),
    )(where, params, *pieces, *fields)


def body(fields, centres, sides, quarters):
    shift = functools.partial(lax.ppermute, axis_name=AX)
    grp = lax.axis_index("grp")
    parity = lax.axis_index("mem") % 2
    where = jnp.stack([grp, parity]).astype(jnp.int32)

    by_col = fields[0].reshape(16, 4, 32, 2, 256)[:, :, :, ::-1, :]
    by_col = by_col.transpose(2, 3, 1, 0, 4).reshape(MEM, 4, 16, 256)
    mine = lax.all_to_all(by_col, "mem", 0, 0, tiled=True)

    small = jnp.concatenate([sides[0, 0], quarters[0, 0]], axis=-1)
    params = shift(lax.all_gather(small, "grp"), perm=flat_perm(lambda m, g: (m ^ 1, g)))

    parts = split_centres(where, centres[0, 0])
    own = [
        parts[0],
        shift(parts[1], perm=CORE),
        shift(parts[2], perm=PAL),
        shift(parts[3], perm=flat_perm(lambda m, g: (m, g ^ 3))),
    ]
    side = [shift(p, perm=SIDE) for p in own]
    cross = [shift(p, perm=CROSS) for p in own]

    near = shift(mine, perm=CORE)
    far = shift(mine, perm=PAL)
    far_near = shift(far, perm=CORE)
    result = apply_transforms(where, params, own + side + cross, [mine, near, far, far_near])

    send = result.reshape(4, 4, MEM, 4, 256).transpose(2, 0, 1, 3, 4).reshape(MEM * GRP, 16, 256)
    got = lax.all_to_all(send, AX, 0, 0, tiled=True)
    got = got.reshape(32, 2, 2, 2, 4, 4, 256)
    got = jnp.stack([got[:, 1, ::-1], got[:, 0]], axis=1)
    return got.transpose(2, 3, 5, 4, 0, 1, 6).reshape(1, 16, 4, MEM, 256)


def solution(mesh):
    return jax.shard_map(
        body,
        mesh=mesh,
        in_specs=(
            P("grp", "mem", None, None, None),
            P("grp", "mem", None, None),
            P("grp", "mem", None, None),
            P("grp", "mem", None, None),
        ),
        out_specs=P("grp", "mem", None, None, None),
        check_vma=False,
    )
```

```python
import functools

import jax
import jax.numpy as jnp
from jax import lax
from jax.experimental import pallas as pl
from jax.experimental.layout import Layout, with_layout_constraint
from jax.experimental.pallas import tpu as pltpu
from jax.sharding import PartitionSpec as P

AX = ("mem", "grp")
MEM = 64
GRP = 4
K = 1024
JQ = 256
JP = JQ + 16
HALF = K // 2
CUT = 192


def flat_perm(move):
    pairs = []
    for mem in range(MEM):
        for grp in range(GRP):
            to_mem, to_grp = move(mem, grp)
            pairs.append((mem * GRP + grp, (to_mem % MEM) * GRP + to_grp))
    return pairs


CORE = flat_perm(lambda m, g: (m, g ^ 1))
PAL = flat_perm(lambda m, g: (m, g ^ 2))
CROSS = flat_perm(lambda m, g: (m ^ 1, g ^ 2))
SIDE = flat_perm(lambda m, g: (m + 2 if m % 2 else m - 2, g))


FIELD_GROUPS = [
    [(c ^ 1) * GRP + 2 * (((c ^ 1) & 1) ^ flank) + core for c in range(MEM)]
    for flank in range(2)
    for core in range(2)
]
RESULT_GROUP = [
    [(c ^ 1) * GRP + (quarter ^ (2 * ((c ^ 1) & 1))) for c in range(MEM) for quarter in range(GRP)]
]
VMEM_LIMIT = 24 * 1024 * 1024
LIGHT = pl.CostEstimate(flops=1, bytes_accessed=1, transcendentals=0)


def split_kernel(where_ref, sides_ref, quarters_ref, centre_ref, keep_ref, mate_ref, far_ref):
    grp = where_ref[0]
    parity = where_ref[1]
    row = lax.broadcasted_iota(jnp.int32, (JQ, K), 0)
    col = lax.broadcasted_iota(jnp.int32, (JQ, K), 1)
    base = lax.bitwise_xor(row // 4, 1) * 16 + row % 4
    lane = lax.broadcasted_iota(jnp.int32, (16, K), 1)
    small = jnp.zeros((16, K), jnp.int32)
    for sub in range(4):
        for n in range(2):
            small = jnp.where(lane == 4 * sub + n, sides_ref[sub, n], small)
            small = jnp.where(lane == 4 * sub + 2 + n, quarters_ref[sub, n], small)
    small = small.astype(jnp.float32).astype(jnp.bfloat16)
    ordered = jnp.concatenate(
        [centre_ref[:, 1].reshape(HALF, K), centre_ref[:, 0].reshape(HALF, K)], axis=0
    )
    for rho, out in enumerate((keep_ref, mate_ref.at[0], far_ref, mate_ref.at[1])):
        quarter = lax.bitwise_xor(lax.bitwise_xor(grp, rho), 2 * parity)
        pick = jnp.where(col == base + 4 * quarter, 1.0, 0.0).astype(jnp.bfloat16)
        out[:JQ, :] = lax.dot_general(
            pick, ordered, (((1,), (1,)), ((), ())), preferred_element_type=jnp.float32
        ).astype(jnp.bfloat16)
        out[JQ:, :] = small


def split_centres(where, sides, quarters, centre):
    smem = pl.BlockSpec(memory_space=pltpu.SMEM)
    vmem = pl.BlockSpec(memory_space=pltpu.VMEM)
    one = jax.ShapeDtypeStruct((JP, K), jnp.bfloat16)
    two = jax.ShapeDtypeStruct((2, JP, K), jnp.bfloat16)
    return pl.pallas_call(
        split_kernel,
        out_shape=[one, two, one],
        in_specs=[smem, smem, smem, vmem],
        out_specs=[vmem] * 3,
        compiler_params=pltpu.CompilerParams(vmem_limit_bytes=VMEM_LIMIT),
        cost_estimate=LIGHT,
    )(where, sides, quarters, centre.reshape(32, 2, 16, K))


def blend_kernel(first, count, where_ref, params_ref, own01, own23, cross01, cross23, side, out_ref, table, sems):
    grp = where_ref[0]
    parity = where_ref[1]
    at = pl.ds(first, count)
    copies = [
        pltpu.make_async_copy(own01.at[:, at], table.at[0:2], sems.at[0]),
        pltpu.make_async_copy(own23.at[:, at], table.at[2:4], sems.at[1]),
        pltpu.make_async_copy(side, table.at[4:8], sems.at[2]),
        pltpu.make_async_copy(cross01.at[:, at], table.at[8:10], sems.at[3]),
        pltpu.make_async_copy(cross23.at[:, at], table.at[10:12], sems.at[4]),
    ]
    for copy in copies:
        copy.start()
    for copy in copies:
        copy.wait()

    @pl.loop(0, 4)
    def _(row):
        i_own = lax.bitwise_xor(lax.bitwise_xor(row, grp), 2)
        for sub in range(4):
            side_row = params_ref[i_own, 4 * sub]
            side_col = params_ref[i_own, 4 * sub + 1]
            a = params_ref[i_own, 4 * sub + 2].astype(jnp.float32) * 0.25
            b = params_ref[i_own, 4 * sub + 3].astype(jnp.float32) * 0.25
            row2 = lax.bitwise_and(row + 2 * side_row - 1, 3)
            base2 = jnp.where(side_col == parity, 0, 4)
            i_row = lax.bitwise_xor(lax.bitwise_xor(row2, grp), 2)
            i_col = base2 + lax.bitwise_xor(row, grp)
            i_diag = base2 + lax.bitwise_xor(row2, grp)
            w_own = (1.0 - a) * (1.0 - b)
            w_row = a * (1.0 - b)
            w_col = (1.0 - a) * b
            w_diag = a * b

            @pl.loop(0, count // 32)
            def _(step):
                at = pl.ds(pl.multiple_of(step * 32, 32), 32)
                mixed = w_own * table[8 + i_own, at, :].astype(jnp.float32)
                mixed = mixed + w_row * table[8 + i_row, at, :].astype(jnp.float32)
                mixed = mixed + w_col * table[i_col, at, :].astype(jnp.float32)
                mixed = mixed + w_diag * table[i_diag, at, :].astype(jnp.float32)
                out_ref[4 * row + sub, at, :] = mixed.astype(jnp.bfloat16)


def blend_centres(where, params, own01, own23, cross01, cross23, side, first, count):
    smem = pl.BlockSpec(memory_space=pltpu.SMEM)
    return pl.pallas_call(
        functools.partial(blend_kernel, first, count),
        out_shape=jax.ShapeDtypeStruct((16, count, K), jnp.bfloat16),
        in_specs=[smem, smem] + [pl.BlockSpec(memory_space=pltpu.HBM)] * 5,
        out_specs=pl.BlockSpec(memory_space=pltpu.VMEM),
        scratch_shapes=[
            pltpu.VMEM((12, count, K), jnp.bfloat16),
            pltpu.SemaphoreType.DMA((5,)),
        ],
        compiler_params=pltpu.CompilerParams(vmem_limit_bytes=VMEM_LIMIT),
        cost_estimate=LIGHT,
    )(where, params, own01, own23, cross01, cross23, side)


def sub_block(product, cols, rows):
    lane = lax.broadcasted_iota(jnp.int32, (rows, 128), 1)
    return jnp.where(lane < 64, product[:rows, cols], product[rows:, cols])


def side_by_side(refs, half, row, at):
    return jnp.concatenate(
        [ref[:, half, pl.ds(row, 1), :, at].reshape(HALF, 128) for ref in refs], axis=1
    )


def here_kernel(blend_ref, mine, near, out_ref):
    @pl.loop(0, 4)
    def _(row):
        for pair in range(2):
            at = slice(pair * 128, pair * 128 + 128)
            for two in range(2):
                half = 1 - two
                left = blend_ref[pl.ds(4 * row + 2 * pair, 2), :, half * HALF : half * HALF + HALF]
                product = jnp.dot(
                    left.reshape(2 * CUT, HALF),
                    side_by_side((mine, near), half, row, at),
                    preferred_element_type=jnp.float32,
                )
                for n in range(2):
                    out_ref[2 * pair + two, n, row] = sub_block(
                        product, slice(n * 128, n * 128 + 128), CUT
                    )


def apply_here(blend, mine, near):
    vmem = pl.BlockSpec(memory_space=pltpu.VMEM)
    return pl.pallas_call(
        here_kernel,
        out_shape=jax.ShapeDtypeStruct((4, 2, 4, CUT, 128), jnp.float32),
        in_specs=[vmem] * 3,
        out_specs=vmem,
        compiler_params=pltpu.CompilerParams(vmem_limit_bytes=VMEM_LIMIT),
        cost_estimate=LIGHT,
    )(blend, mine.reshape(32, 2, 4, 16, 256), near.reshape(32, 2, 4, 16, 256))


def apply_kernel(where_ref, blend_a, blend_b, part, mine, near, far, far_near, out_ref, total):
    quarter = where_ref[2]

    @pl.loop(0, 4)
    def _(row):
        for pair in range(2):
            at = slice(pair * 128, pair * 128 + 128)
            subs = pl.ds(4 * row + 2 * pair, 2)
            for two in range(2):
                there = side_by_side((far, far_near), two, row, at)
                here = side_by_side((mine, near), 1 - two, row, at)
                both = (there, here) if two == 0 else (here, there)
                top = jnp.dot(
                    blend_a[subs, :, two * HALF : two * HALF + HALF].reshape(2 * CUT, HALF),
                    there,
                    preferred_element_type=jnp.float32,
                )
                rest = jnp.dot(
                    blend_b[subs].reshape(2 * (JQ - CUT), K),
                    jnp.concatenate(both, axis=0),
                    preferred_element_type=jnp.float32,
                )
                for n in range(2):
                    cols = slice(n * 128, n * 128 + 128)
                    to = (pair, 2 * two + n)
                    total[(*to, pl.ds(row, CUT, stride=4), slice(None))] = (
                        sub_block(top, cols, CUT) + part[2 * pair + two, n, row]
                    )
                    total[(*to, pl.ds(row + 4 * CUT, JQ - CUT, stride=4), slice(None))] = (
                        sub_block(rest, cols, JQ - CUT)
                    )

    for rho in range(4):
        level = lax.bitwise_xor(quarter, rho)
        for pair in range(2):
            at = slice(pair * 128, pair * 128 + 128)
            done = total[pair, rho].reshape(32, 2, 16, 128).astype(jnp.bfloat16)
            out_ref[:, 0, lax.bitwise_xor(level, 2), :, at] = done[:, 0]
            out_ref[:, 1, level, :, at] = done[:, 1]


def apply_transforms(where, blend_a, blend_b, part, fields):
    vmem = pl.BlockSpec(memory_space=pltpu.VMEM)
    return pl.pallas_call(
        apply_kernel,
        out_shape=jax.ShapeDtypeStruct((32, 2, 4, 16, 256), jnp.bfloat16),
        in_specs=[pl.BlockSpec(memory_space=pltpu.SMEM)] + [vmem] * 7,
        out_specs=vmem,
        scratch_shapes=[pltpu.VMEM((2, 4, 4 * JQ, 128), jnp.float32)],
        compiler_params=pltpu.CompilerParams(vmem_limit_bytes=VMEM_LIMIT),
        cost_estimate=LIGHT,
    )(where, blend_a, blend_b, part, *(f.reshape(32, 2, 4, 16, 256) for f in fields))


def body(fields, centres, sides, quarters):
    shift = functools.partial(lax.ppermute, axis_name=AX)
    grp = lax.axis_index("grp")
    parity = lax.bitwise_and(lax.axis_index("mem"), 1)
    where = jnp.stack([grp, parity, lax.bitwise_xor(grp, 2 * parity)]).astype(jnp.int32)

    by_col = with_layout_constraint(
        fields[0].transpose(2, 1, 0, 3), Layout(major_to_minor=(0, 1, 2, 3))
    )
    mine = lax.all_to_all(by_col, AX, 0, 0, axis_index_groups=FIELD_GROUPS, tiled=True)

    keep, to_mate, to_far = split_centres(where, sides[0, 0], quarters[0, 0], centres[0, 0])
    mate = shift(to_mate, perm=CORE)
    own23 = shift(jnp.stack([to_far, mate[1]]), perm=PAL)
    own01 = jnp.stack([keep, mate[0]])
    cross01 = shift(own01, perm=CROSS)
    own_a = jnp.concatenate([own01[:, :CUT], own23[:, :CUT]])
    own_b = jnp.concatenate([own01[:, CUT:JQ], own23[:, CUT:JQ]])
    mine, own01, own23, own_a, own_b, cross01 = lax.optimization_barrier(
        (mine, own01, own23, own_a, own_b, cross01)
    )

    far = shift(mine, perm=PAL)
    side_a = shift(own_a, perm=SIDE)
    cross23 = shift(own23, perm=CROSS)
    side_b = shift(own_b, perm=SIDE)
    near = shift(mine, perm=CORE)
    params = jnp.concatenate([cross01[:, JQ, :16], cross23[:, JQ, :16]]).astype(jnp.int32)
    four = (own01, own23, cross01, cross23)
    blend_a = blend_centres(where, params, *four, side_a, 0, CUT)
    part = apply_here(blend_a, mine, near)
    far, part, side_b = lax.optimization_barrier((far, part, side_b))
    far_near = shift(far, perm=CORE)
    blend_b = blend_centres(where, params, *four, side_b, CUT, JQ - CUT)
    result = apply_transforms(where, blend_a, blend_b, part, (mine, near, far, far_near))

    got = lax.all_to_all(
        result.reshape(MEM * GRP, 16, 256), AX, 0, 0, axis_index_groups=RESULT_GROUP, tiled=True
    )
    return got.reshape(MEM, 64, 256).transpose(1, 0, 2).reshape(1, 16, 4, MEM, 256)


def solution(mesh):
    return jax.shard_map(
        body,
        mesh=mesh,
        in_specs=(
            P("grp", "mem", None, None, None),
            P("grp", "mem", None, None),
            P("grp", "mem", None, None),
            P("grp", "mem", None, None),
        ),
        out_specs=P("grp", "mem", None, None, None),
        check_vma=False,
    )
```

```python
import functools

import jax
import jax.numpy as jnp
from jax import lax
from jax.experimental import pallas as pl
from jax.experimental.layout import Layout, with_layout_constraint
from jax.experimental.pallas import tpu as pltpu
from jax.sharding import PartitionSpec as P

AX = ("mem", "grp")
MEM = 64
GRP = 4
K = 1024
JQ = 256
JP = JQ + 16
HALF = K // 2
CUT = 176


def flat_perm(move):
    pairs = []
    for mem in range(MEM):
        for grp in range(GRP):
            to_mem, to_grp = move(mem, grp)
            pairs.append((mem * GRP + grp, (to_mem % MEM) * GRP + to_grp))
    return pairs


CORE = flat_perm(lambda m, g: (m, g ^ 1))
PAL = flat_perm(lambda m, g: (m, g ^ 2))
CROSS = flat_perm(lambda m, g: (m ^ 1, g ^ 2))
SIDE = flat_perm(lambda m, g: (m + 2 if m % 2 else m - 2, g))


FIELD_GROUPS = [
    [(c ^ 1) * GRP + 2 * (((c ^ 1) & 1) ^ flank) + core for c in range(MEM)]
    for flank in range(2)
    for core in range(2)
]
RESULT_GROUP = [
    [(c ^ 1) * GRP + (quarter ^ (2 * ((c ^ 1) & 1))) for c in range(MEM) for quarter in range(GRP)]
]
VMEM_LIMIT = 24 * 1024 * 1024
LIGHT = pl.CostEstimate(flops=1, bytes_accessed=1, transcendentals=0)


def split_kernel(where_ref, sides_ref, quarters_ref, centre_ref, keep_ref, mate_ref, far_ref):
    grp = where_ref[0]
    parity = where_ref[1]
    row = lax.broadcasted_iota(jnp.int32, (JQ, K), 0)
    col = lax.broadcasted_iota(jnp.int32, (JQ, K), 1)
    base = lax.bitwise_xor(row // 4, 1) * 16 + row % 4
    lane = lax.broadcasted_iota(jnp.int32, (16, K), 1)
    small = jnp.zeros((16, K), jnp.int32)
    for sub in range(4):
        for n in range(2):
            small = jnp.where(lane == 4 * sub + n, sides_ref[sub, n], small)
            small = jnp.where(lane == 4 * sub + 2 + n, quarters_ref[sub, n], small)
    small = small.astype(jnp.float32).astype(jnp.bfloat16)
    ordered = jnp.concatenate(
        [centre_ref[:, 1].reshape(HALF, K), centre_ref[:, 0].reshape(HALF, K)], axis=0
    )
    for rho, out in enumerate((keep_ref, mate_ref.at[0], far_ref, mate_ref.at[1])):
        quarter = lax.bitwise_xor(lax.bitwise_xor(grp, rho), 2 * parity)
        pick = jnp.where(col == base + 4 * quarter, 1.0, 0.0).astype(jnp.bfloat16)
        out[:JQ, :] = lax.dot_general(
            pick, ordered, (((1,), (1,)), ((), ())), preferred_element_type=jnp.float32
        ).astype(jnp.bfloat16)
        out[JQ:, :] = small


def split_centres(where, sides, quarters, centre):
    smem = pl.BlockSpec(memory_space=pltpu.SMEM)
    vmem = pl.BlockSpec(memory_space=pltpu.VMEM)
    one = jax.ShapeDtypeStruct((JP, K), jnp.bfloat16)
    two = jax.ShapeDtypeStruct((2, JP, K), jnp.bfloat16)
    return pl.pallas_call(
        split_kernel,
        out_shape=[one, two, one],
        in_specs=[smem, smem, smem, vmem],
        out_specs=[vmem] * 3,
        compiler_params=pltpu.CompilerParams(vmem_limit_bytes=VMEM_LIMIT),
        cost_estimate=LIGHT,
    )(where, sides, quarters, centre.reshape(32, 2, 16, K))


def blend_kernel(first, count, where_ref, params_ref, own, side, cross0, cross123, out_ref, table, sems):
    grp = where_ref[0]
    parity = where_ref[1]
    at = pl.ds(first, count)
    ends = (
        (own, table.at[0:4]),
        (side, table.at[4:8]),
        (cross0.at[at], table.at[8]),
        (cross123.at[:, at], table.at[9:12]),
    )
    copies = [pltpu.make_async_copy(a, b, sems.at[n]) for n, (a, b) in enumerate(ends)]
    for copy in copies:
        copy.start()
    for copy in copies:
        copy.wait()

    @pl.loop(0, 4)
    def _(row):
        i_own = lax.bitwise_xor(lax.bitwise_xor(row, grp), 2)
        plans = []
        for sub in range(4):
            side_row = params_ref[i_own, 4 * sub]
            side_col = params_ref[i_own, 4 * sub + 1]
            a = params_ref[i_own, 4 * sub + 2].astype(jnp.float32) * 0.25
            b = params_ref[i_own, 4 * sub + 3].astype(jnp.float32) * 0.25
            row2 = lax.bitwise_and(row + 2 * side_row - 1, 3)
            base2 = jnp.where(side_col == parity, 0, 4)
            i_row = 8 + lax.bitwise_xor(lax.bitwise_xor(row2, grp), 2)
            i_col = base2 + lax.bitwise_xor(row, grp)
            i_diag = base2 + lax.bitwise_xor(row2, grp)
            terms = ((a * (1.0 - b), i_row), ((1.0 - a) * b, i_col), (a * b, i_diag))
            plans.append(((1.0 - a) * (1.0 - b), terms))

        @pl.loop(0, count // 16)
        def _(step):
            at = pl.ds(pl.multiple_of(step * 16, 16), 16)
            own_part = table[8 + i_own, at, :].astype(jnp.float32)
            for sub, (weight, terms) in enumerate(plans):
                mixed = weight * own_part
                for share, index in terms:
                    mixed = mixed + share * table[index, at, :].astype(jnp.float32)
                out_ref[4 * row + sub, at, :] = mixed.astype(jnp.bfloat16)


def blend_centres(where, params, own, side, cross0, cross123, first, count):
    smem = pl.BlockSpec(memory_space=pltpu.SMEM)
    return pl.pallas_call(
        functools.partial(blend_kernel, first, count),
        out_shape=jax.ShapeDtypeStruct((16, count, K), jnp.bfloat16),
        in_specs=[smem, smem] + [pl.BlockSpec(memory_space=pltpu.HBM)] * 4,
        out_specs=pl.BlockSpec(memory_space=pltpu.VMEM),
        scratch_shapes=[
            pltpu.VMEM((12, count, K), jnp.bfloat16),
            pltpu.SemaphoreType.DMA((4,)),
        ],
        compiler_params=pltpu.CompilerParams(vmem_limit_bytes=VMEM_LIMIT),
        cost_estimate=LIGHT,
    )(where, params, own, side, cross0, cross123)


def sub_block(product, cols, rows):
    lane = lax.broadcasted_iota(jnp.int32, (rows, 128), 1)
    return jnp.where(lane < 64, product[:rows, cols], product[rows:, cols])


def side_by_side(refs, half, row, at):
    return jnp.concatenate(
        [ref[:, half, pl.ds(row, 1), :, at].reshape(HALF, 128) for ref in refs], axis=1
    )


def here_kernel(blend_ref, mine, near, out_ref):
    @pl.loop(0, 4)
    def _(row):
        for pair in range(2):
            at = slice(pair * 128, pair * 128 + 128)
            for two in range(2):
                half = 1 - two
                left = blend_ref[pl.ds(4 * row + 2 * pair, 2), :, half * HALF : half * HALF + HALF]
                product = jnp.dot(
                    left.reshape(2 * CUT, HALF),
                    side_by_side((mine, near), half, row, at),
                    preferred_element_type=jnp.float32,
                )
                for n in range(2):
                    out_ref[2 * pair + two, n, row] = sub_block(
                        product, slice(n * 128, n * 128 + 128), CUT
                    )


def apply_here(blend, mine, near):
    vmem = pl.BlockSpec(memory_space=pltpu.VMEM)
    return pl.pallas_call(
        here_kernel,
        out_shape=jax.ShapeDtypeStruct((4, 2, 4, CUT, 128), jnp.float32),
        in_specs=[vmem] * 3,
        out_specs=vmem,
        compiler_params=pltpu.CompilerParams(vmem_limit_bytes=VMEM_LIMIT),
        cost_estimate=LIGHT,
    )(blend, mine.reshape(32, 2, 4, 16, 256), near.reshape(32, 2, 4, 16, 256))


def apply_kernel(where_ref, blend_a, blend_b, part, mine, near, far, far_near, out_ref, total):
    quarter = where_ref[2]

    @pl.loop(0, 4)
    def _(row):
        for pair in range(2):
            at = slice(pair * 128, pair * 128 + 128)
            subs = pl.ds(4 * row + 2 * pair, 2)
            for two in range(2):
                there = side_by_side((far, far_near), two, row, at)
                here = side_by_side((mine, near), 1 - two, row, at)
                both = (there, here) if two == 0 else (here, there)
                top = jnp.dot(
                    blend_a[subs, :, two * HALF : two * HALF + HALF].reshape(2 * CUT, HALF),
                    there,
                    preferred_element_type=jnp.float32,
                )
                rest = jnp.dot(
                    blend_b[subs].reshape(2 * (JQ - CUT), K),
                    jnp.concatenate(both, axis=0),
                    preferred_element_type=jnp.float32,
                )
                for n in range(2):
                    cols = slice(n * 128, n * 128 + 128)
                    to = (pair, 2 * two + n)
                    total[(*to, pl.ds(row, CUT, stride=4), slice(None))] = (
                        sub_block(top, cols, CUT) + part[2 * pair + two, n, row]
                    )
                    total[(*to, pl.ds(row + 4 * CUT, JQ - CUT, stride=4), slice(None))] = (
                        sub_block(rest, cols, JQ - CUT)
                    )

    for rho in range(4):
        level = lax.bitwise_xor(quarter, rho)
        for pair in range(2):
            at = slice(pair * 128, pair * 128 + 128)
            done = total[pair, rho].reshape(32, 2, 16, 128).astype(jnp.bfloat16)
            out_ref[:, 0, lax.bitwise_xor(level, 2), :, at] = done[:, 0]
            out_ref[:, 1, level, :, at] = done[:, 1]


def apply_transforms(where, blend_a, blend_b, part, fields):
    vmem = pl.BlockSpec(memory_space=pltpu.VMEM)
    return pl.pallas_call(
        apply_kernel,
        out_shape=jax.ShapeDtypeStruct((32, 2, 4, 16, 256), jnp.bfloat16),
        in_specs=[pl.BlockSpec(memory_space=pltpu.SMEM)] + [vmem] * 7,
        out_specs=vmem,
        scratch_shapes=[pltpu.VMEM((2, 4, 4 * JQ, 128), jnp.float32)],
        compiler_params=pltpu.CompilerParams(vmem_limit_bytes=VMEM_LIMIT),
        cost_estimate=LIGHT,
    )(where, blend_a, blend_b, part, *(f.reshape(32, 2, 4, 16, 256) for f in fields))


def body(fields, centres, sides, quarters):
    shift = functools.partial(lax.ppermute, axis_name=AX)
    grp = lax.axis_index("grp")
    parity = lax.bitwise_and(lax.axis_index("mem"), 1)
    where = jnp.stack([grp, parity, lax.bitwise_xor(grp, 2 * parity)]).astype(jnp.int32)

    by_col = with_layout_constraint(
        fields[0].transpose(2, 1, 0, 3), Layout(major_to_minor=(0, 1, 2, 3))
    )
    mine = lax.all_to_all(by_col, AX, 0, 0, axis_index_groups=FIELD_GROUPS, tiled=True)

    keep, to_mate, to_far = split_centres(where, sides[0, 0], quarters[0, 0], centres[0, 0])
    mate = shift(to_mate, perm=CORE)
    own23 = shift(jnp.stack([to_far, mate[1]]), perm=PAL)
    cross0 = shift(keep, perm=CROSS)
    own_a = jnp.concatenate([keep[None, :CUT], mate[:1, :CUT], own23[:, :CUT]])
    own_b = jnp.concatenate([keep[None, CUT:JQ], mate[:1, CUT:JQ], own23[:, CUT:JQ]])
    own123 = jnp.concatenate([mate[:1], own23])
    mine, own123, own_a, own_b, cross0 = lax.optimization_barrier(
        (mine, own123, own_a, own_b, cross0)
    )

    far = shift(mine, perm=PAL)
    side_a = shift(own_a, perm=SIDE)
    cross123 = shift(own123, perm=CROSS)
    side_b = shift(own_b, perm=SIDE)
    near = shift(mine, perm=CORE)
    params = jnp.concatenate([cross0[JQ : JQ + 1, :16], cross123[:, JQ, :16]]).astype(jnp.int32)
    blend_a = blend_centres(where, params, own_a, side_a, cross0, cross123, 0, CUT)
    part = apply_here(blend_a, mine, near)
    far, part, side_b = lax.optimization_barrier((far, part, side_b))
    far_near = shift(far, perm=CORE)
    blend_b = blend_centres(where, params, own_b, side_b, cross0, cross123, CUT, JQ - CUT)
    result = apply_transforms(where, blend_a, blend_b, part, (mine, near, far, far_near))

    got = lax.all_to_all(
        result.reshape(MEM * GRP, 16, 256), AX, 0, 0, axis_index_groups=RESULT_GROUP, tiled=True
    )
    return got.reshape(MEM, 64, 256).transpose(1, 0, 2).reshape(1, 16, 4, MEM, 256)


def solution(mesh):
    return jax.shard_map(
        body,
        mesh=mesh,
        in_specs=(
            P("grp", "mem", None, None, None),
            P("grp", "mem", None, None),
            P("grp", "mem", None, None),
            P("grp", "mem", None, None),
        ),
        out_specs=P("grp", "mem", None, None, None),
        check_vma=False,
    )
```

```python
import functools

import jax
import jax.numpy as jnp
from jax import lax
from jax.experimental import pallas as pl
from jax.experimental.layout import Layout, with_layout_constraint
from jax.experimental.pallas import tpu as pltpu
from jax.sharding import PartitionSpec as P

AX = ("mem", "grp")
MEM = 64
GRP = 4
K = 1024
JQ = 256
JP = JQ + 16
HALF = K // 2
CUT = 192


def flat_perm(move):
    pairs = []
    for mem in range(MEM):
        for grp in range(GRP):
            to_mem, to_grp = move(mem, grp)
            pairs.append((mem * GRP + grp, (to_mem % MEM) * GRP + to_grp))
    return pairs


CORE = flat_perm(lambda m, g: (m, g ^ 1))
PAL = flat_perm(lambda m, g: (m, g ^ 2))
CROSS = flat_perm(lambda m, g: (m ^ 1, g ^ 2))
SIDE = flat_perm(lambda m, g: (m + 2 if m % 2 else m - 2, g))


FIELD_GROUPS = [
    [(c ^ 1) * GRP + 2 * (((c ^ 1) & 1) ^ flank) + core for c in range(MEM)]
    for flank in range(2)
    for core in range(2)
]
RESULT_GROUP = [
    [(c ^ 1) * GRP + (quarter ^ (2 * ((c ^ 1) & 1))) for quarter in range(GRP) for c in range(MEM)]
]
VMEM_LIMIT = 24 * 1024 * 1024
LIGHT = pl.CostEstimate(flops=1, bytes_accessed=1, transcendentals=0)


def split_kernel(where_ref, sides_ref, quarters_ref, centre_ref, keep_ref, mate_ref, far_ref):
    grp = where_ref[0]
    parity = where_ref[1]
    row = lax.broadcasted_iota(jnp.int32, (JQ, K), 0)
    col = lax.broadcasted_iota(jnp.int32, (JQ, K), 1)
    base = lax.bitwise_xor(row // 4, 1) * 16 + row % 4
    lane = lax.broadcasted_iota(jnp.int32, (16, K), 1)
    small = jnp.zeros((16, K), jnp.int32)
    for sub in range(4):
        for n in range(2):
            small = jnp.where(lane == 4 * sub + n, sides_ref[sub, n], small)
            small = jnp.where(lane == 4 * sub + 2 + n, quarters_ref[sub, n], small)
    small = small.astype(jnp.float32).astype(jnp.bfloat16)
    ordered = jnp.concatenate(
        [centre_ref[:, 1].reshape(HALF, K), centre_ref[:, 0].reshape(HALF, K)], axis=0
    )
    for rho, out in enumerate((keep_ref, mate_ref.at[0], far_ref, mate_ref.at[1])):
        quarter = lax.bitwise_xor(lax.bitwise_xor(grp, rho), 2 * parity)
        pick = jnp.where(col == base + 4 * quarter, 1.0, 0.0).astype(jnp.bfloat16)
        out[:JQ, :] = lax.dot_general(
            pick, ordered, (((1,), (1,)), ((), ())), preferred_element_type=jnp.float32
        ).astype(jnp.bfloat16)
        out[JQ:, :] = small


def split_centres(where, sides, quarters, centre):
    smem = pl.BlockSpec(memory_space=pltpu.SMEM)
    vmem = pl.BlockSpec(memory_space=pltpu.VMEM)
    one = jax.ShapeDtypeStruct((JP, K), jnp.bfloat16)
    two = jax.ShapeDtypeStruct((2, JP, K), jnp.bfloat16)
    return pl.pallas_call(
        split_kernel,
        out_shape=[one, two, one],
        in_specs=[smem, smem, smem, vmem],
        out_specs=[vmem] * 3,
        compiler_params=pltpu.CompilerParams(vmem_limit_bytes=VMEM_LIMIT),
        cost_estimate=LIGHT,
    )(where, sides, quarters, centre.reshape(32, 2, 16, K))


def blend_kernel(first, count, where_ref, params_ref, own, side, cross0, cross123, out_ref, table, sems):
    grp = where_ref[0]
    parity = where_ref[1]
    at = pl.ds(first, count)
    ends = (
        (own, table.at[0:4]),
        (side, table.at[4:8]),
        (cross0.at[at], table.at[8]),
        (cross123.at[:, at], table.at[9:12]),
    )
    copies = [pltpu.make_async_copy(a, b, sems.at[n]) for n, (a, b) in enumerate(ends)]
    for copy in copies:
        copy.start()
    for copy in copies:
        copy.wait()

    @pl.loop(0, 4)
    def _(row):
        i_own = lax.bitwise_xor(lax.bitwise_xor(row, grp), 2)
        plans = []
        for sub in range(4):
            side_row = params_ref[i_own, 4 * sub]
            side_col = params_ref[i_own, 4 * sub + 1]
            a = params_ref[i_own, 4 * sub + 2].astype(jnp.float32) * 0.25
            b = params_ref[i_own, 4 * sub + 3].astype(jnp.float32) * 0.25
            row2 = lax.bitwise_and(row + 2 * side_row - 1, 3)
            base2 = jnp.where(side_col == parity, 0, 4)
            i_row = 8 + lax.bitwise_xor(lax.bitwise_xor(row2, grp), 2)
            i_col = base2 + lax.bitwise_xor(row, grp)
            i_diag = base2 + lax.bitwise_xor(row2, grp)
            terms = ((a * (1.0 - b), i_row), ((1.0 - a) * b, i_col), (a * b, i_diag))
            plans.append(((1.0 - a) * (1.0 - b), terms))

        @pl.loop(0, count // 16)
        def _(step):
            at = pl.ds(pl.multiple_of(step * 16, 16), 16)
            own_part = table[8 + i_own, at, :].astype(jnp.float32)
            for sub, (weight, terms) in enumerate(plans):
                mixed = weight * own_part
                for share, index in terms:
                    mixed = mixed + share * table[index, at, :].astype(jnp.float32)
                out_ref[4 * row + sub, at, :] = mixed.astype(jnp.bfloat16)


def blend_centres(where, params, own, side, cross0, cross123, first, count):
    smem = pl.BlockSpec(memory_space=pltpu.SMEM)
    return pl.pallas_call(
        functools.partial(blend_kernel, first, count),
        out_shape=jax.ShapeDtypeStruct((16, count, K), jnp.bfloat16),
        in_specs=[smem, smem] + [pl.BlockSpec(memory_space=pltpu.HBM)] * 4,
        out_specs=pl.BlockSpec(memory_space=pltpu.VMEM),
        scratch_shapes=[
            pltpu.VMEM((12, count, K), jnp.bfloat16),
            pltpu.SemaphoreType.DMA((4,)),
        ],
        compiler_params=pltpu.CompilerParams(vmem_limit_bytes=VMEM_LIMIT),
        cost_estimate=LIGHT,
    )(where, params, own, side, cross0, cross123)


def sub_block(product, cols, rows):
    lane = lax.broadcasted_iota(jnp.int32, (rows, 128), 1)
    return jnp.where(lane < 64, product[:rows, cols], product[rows:, cols])


def side_by_side(refs, half, row, at):
    return jnp.concatenate(
        [ref[:, half, pl.ds(row, 1), :, at].reshape(HALF, 128) for ref in refs], axis=1
    )


def here_kernel(blend_ref, mine, near, out_ref):
    count = blend_ref.shape[1]

    @pl.loop(0, 4)
    def _(row):
        for pair in range(2):
            at = slice(pair * 128, pair * 128 + 128)
            for two in range(2):
                half = 1 - two
                left = blend_ref[pl.ds(4 * row + 2 * pair, 2), :, half * HALF : half * HALF + HALF]
                product = jnp.dot(
                    left.reshape(2 * count, HALF),
                    side_by_side((mine, near), half, row, at),
                    preferred_element_type=jnp.float32,
                )
                for n in range(2):
                    out_ref[2 * pair + two, n, row] = sub_block(
                        product, slice(n * 128, n * 128 + 128), count
                    )


def apply_here(blend, mine, near):
    vmem = pl.BlockSpec(memory_space=pltpu.VMEM)
    return pl.pallas_call(
        here_kernel,
        out_shape=jax.ShapeDtypeStruct((4, 2, 4, blend.shape[1], 128), jnp.float32),
        in_specs=[vmem] * 3,
        out_specs=vmem,
        compiler_params=pltpu.CompilerParams(vmem_limit_bytes=VMEM_LIMIT),
        cost_estimate=LIGHT,
    )(blend, mine.reshape(32, 2, 4, 16, 256), near.reshape(32, 2, 4, 16, 256))


def apply_kernel(where_ref, blend_a, blend_b, part_a, part_b, far, far_near, out_ref, total):
    quarter = where_ref[2]
    rest = JQ - CUT

    @pl.loop(0, 4)
    def _(row):
        for pair in range(2):
            at = slice(pair * 128, pair * 128 + 128)
            subs = pl.ds(4 * row + 2 * pair, 2)
            for two in range(2):
                lanes = slice(two * HALF, two * HALF + HALF)
                left = jnp.concatenate(
                    [
                        blend_a[subs, :, lanes].reshape(2 * CUT, HALF),
                        blend_b[subs, :, lanes].reshape(2 * rest, HALF),
                    ],
                    axis=0,
                )
                product = jnp.dot(
                    left,
                    side_by_side((far, far_near), two, row, at),
                    preferred_element_type=jnp.float32,
                )
                for n in range(2):
                    cols = slice(n * 128, n * 128 + 128)
                    to = (pair, 2 * two + n)
                    total[(*to, pl.ds(row, CUT, stride=4), slice(None))] = (
                        sub_block(product[: 2 * CUT], cols, CUT) + part_a[2 * pair + two, n, row]
                    )
                    total[(*to, pl.ds(row + 4 * CUT, rest, stride=4), slice(None))] = (
                        sub_block(product[2 * CUT :], cols, rest) + part_b[2 * pair + two, n, row]
                    )

    for rho in range(4):
        level = lax.bitwise_xor(quarter, rho)
        for pair in range(2):
            at = slice(pair * 128, pair * 128 + 128)
            done = total[pair, rho].reshape(32, 2, 16, 128).astype(jnp.bfloat16)
            out_ref[lax.bitwise_xor(level, 2), :, 0, :, at] = done[:, 0]
            out_ref[level, :, 1, :, at] = done[:, 1]


def apply_transforms(where, blend_a, blend_b, part_a, part_b, fields):
    vmem = pl.BlockSpec(memory_space=pltpu.VMEM)
    return pl.pallas_call(
        apply_kernel,
        out_shape=jax.ShapeDtypeStruct((4, 32, 2, 16, 256), jnp.bfloat16),
        in_specs=[pl.BlockSpec(memory_space=pltpu.SMEM)] + [vmem] * 6,
        out_specs=vmem,
        scratch_shapes=[pltpu.VMEM((2, 4, 4 * JQ, 128), jnp.float32)],
        compiler_params=pltpu.CompilerParams(vmem_limit_bytes=VMEM_LIMIT),
        cost_estimate=LIGHT,
    )(where, blend_a, blend_b, part_a, part_b, *(f.reshape(32, 2, 4, 16, 256) for f in fields))


def body(fields, centres, sides, quarters):
    shift = functools.partial(lax.ppermute, axis_name=AX)
    grp = lax.axis_index("grp")
    parity = lax.bitwise_and(lax.axis_index("mem"), 1)
    where = jnp.stack([grp, parity, lax.bitwise_xor(grp, 2 * parity)]).astype(jnp.int32)

    by_col = with_layout_constraint(
        fields[0].transpose(2, 1, 0, 3), Layout(major_to_minor=(0, 1, 2, 3))
    )
    mine = lax.all_to_all(by_col, AX, 0, 0, axis_index_groups=FIELD_GROUPS, tiled=True)

    keep, to_mate, to_far = split_centres(where, sides[0, 0], quarters[0, 0], centres[0, 0])
    mate = shift(to_mate, perm=CORE)
    own23 = shift(jnp.stack([to_far, mate[1]]), perm=PAL)
    cross0 = shift(keep, perm=CROSS)
    own_a = jnp.concatenate([keep[None, :CUT], mate[:1, :CUT], own23[:, :CUT]])
    own_b = jnp.concatenate([keep[None, CUT:JQ], mate[:1, CUT:JQ], own23[:, CUT:JQ]])
    own123 = jnp.concatenate([mate[:1], own23])
    mine, own123, own_a, own_b, cross0 = lax.optimization_barrier(
        (mine, own123, own_a, own_b, cross0)
    )

    far = shift(mine, perm=PAL)
    side_a = shift(own_a, perm=SIDE)
    cross123 = shift(own123, perm=CROSS)
    side_b = shift(own_b, perm=SIDE)
    near = shift(mine, perm=CORE)
    params = jnp.concatenate([cross0[JQ : JQ + 1, :16], cross123[:, JQ, :16]]).astype(jnp.int32)
    blend_a = blend_centres(where, params, own_a, side_a, cross0, cross123, 0, CUT)
    part_a = apply_here(blend_a, mine, near)
    far, part_a, side_b = lax.optimization_barrier((far, part_a, side_b))
    far_near = shift(far, perm=CORE)
    blend_b = blend_centres(where, params, own_b, side_b, cross0, cross123, CUT, JQ - CUT)
    part_b = apply_here(blend_b, mine, near)
    result = apply_transforms(where, blend_a, blend_b, part_a, part_b, (far, far_near))

    got = lax.all_to_all(
        result.reshape(MEM * GRP, 16, 256), AX, 0, 0, axis_index_groups=RESULT_GROUP, tiled=True
    )
    return got.reshape(GRP, MEM, 16, 256).transpose(0, 2, 1, 3).reshape(1, 16, 4, MEM, 256)


def solution(mesh):
    return jax.shard_map(
        body,
        mesh=mesh,
        in_specs=(
            P("grp", "mem", None, None, None),
            P("grp", "mem", None, None),
            P("grp", "mem", None, None),
            P("grp", "mem", None, None),
        ),
        out_specs=P("grp", "mem", None, None, None),
        check_vma=False,
    )
```

```python
import functools

import jax
import jax.numpy as jnp
from jax import lax
from jax.experimental import pallas as pl
from jax.experimental.layout import Layout, with_layout_constraint
from jax.experimental.pallas import tpu as pltpu
from jax.sharding import PartitionSpec as P

AX = ("mem", "grp")
MEM = 64
GRP = 4
K = 1024
JQ = 256
JP = JQ + 16
HALF = K // 2
CUT = 192


def flat_perm(move):
    pairs = []
    for mem in range(MEM):
        for grp in range(GRP):
            to_mem, to_grp = move(mem, grp)
            pairs.append((mem * GRP + grp, (to_mem % MEM) * GRP + to_grp))
    return pairs


CORE = flat_perm(lambda m, g: (m, g ^ 1))
PAL = flat_perm(lambda m, g: (m, g ^ 2))
CROSS = flat_perm(lambda m, g: (m ^ 1, g ^ 2))
SIDE = flat_perm(lambda m, g: (m + 2 if m % 2 else m - 2, g))


FIELD_GROUPS = [
    [(c ^ 1) * GRP + 2 * (((c ^ 1) & 1) ^ flank) + core for c in range(MEM)]
    for flank in range(2)
    for core in range(2)
]
RESULT_GROUP = [
    [(c ^ 1) * GRP + (quarter ^ (2 * ((c ^ 1) & 1))) for quarter in range(GRP) for c in range(MEM)]
]
VMEM_LIMIT = 24 * 1024 * 1024
LIGHT = pl.CostEstimate(flops=1, bytes_accessed=1, transcendentals=0)


def split_kernel(where_ref, sides_ref, quarters_ref, centre_ref, keep_ref, mate_ref, far_ref):
    grp = where_ref[0]
    parity = where_ref[1]
    row = lax.broadcasted_iota(jnp.int32, (JQ, K), 0)
    col = lax.broadcasted_iota(jnp.int32, (JQ, K), 1)
    base = lax.bitwise_xor(row // 4, 1) * 16 + row % 4
    lane = lax.broadcasted_iota(jnp.int32, (16, K), 1)
    small = jnp.zeros((16, K), jnp.int32)
    for sub in range(4):
        for n in range(2):
            small = jnp.where(lane == 4 * sub + n, sides_ref[sub, n], small)
            small = jnp.where(lane == 4 * sub + 2 + n, quarters_ref[sub, n], small)
    small = small.astype(jnp.float32).astype(jnp.bfloat16)
    ordered = jnp.concatenate(
        [centre_ref[:, 1].reshape(HALF, K), centre_ref[:, 0].reshape(HALF, K)], axis=0
    )
    for rho, out in enumerate((keep_ref, mate_ref.at[0], far_ref, mate_ref.at[1])):
        quarter = lax.bitwise_xor(lax.bitwise_xor(grp, rho), 2 * parity)
        pick = jnp.where(col == base + 4 * quarter, 1.0, 0.0).astype(jnp.bfloat16)
        out[:JQ, :] = lax.dot_general(
            pick, ordered, (((1,), (1,)), ((), ())), preferred_element_type=jnp.float32
        ).astype(jnp.bfloat16)
        out[JQ:, :] = small


def split_centres(where, sides, quarters, centre):
    smem = pl.BlockSpec(memory_space=pltpu.SMEM)
    vmem = pl.BlockSpec(memory_space=pltpu.VMEM)
    one = jax.ShapeDtypeStruct((JP, K), jnp.bfloat16)
    two = jax.ShapeDtypeStruct((2, JP, K), jnp.bfloat16)
    return pl.pallas_call(
        split_kernel,
        out_shape=[one, two, one],
        in_specs=[smem, smem, smem, vmem],
        out_specs=[vmem] * 3,
        compiler_params=pltpu.CompilerParams(vmem_limit_bytes=VMEM_LIMIT),
        cost_estimate=LIGHT,
    )(where, sides, quarters, centre.reshape(32, 2, 16, K))


def blend_kernel(first, count, where_ref, params_ref, own, side, cross0, cross123, out_ref, table, sems):
    grp = where_ref[0]
    parity = where_ref[1]
    at = pl.ds(first, count)
    ends = (
        (own, table.at[0:4]),
        (side, table.at[4:8]),
        (cross0.at[at], table.at[8]),
        (cross123.at[:, at], table.at[9:12]),
    )
    copies = [pltpu.make_async_copy(a, b, sems.at[n]) for n, (a, b) in enumerate(ends)]
    for copy in copies:
        copy.start()
    for copy in copies:
        copy.wait()

    @pl.loop(0, 4)
    def _(row):
        i_own = lax.bitwise_xor(lax.bitwise_xor(row, grp), 2)
        plans = []
        for sub in range(4):
            side_row = params_ref[i_own, 4 * sub]
            side_col = params_ref[i_own, 4 * sub + 1]
            a = params_ref[i_own, 4 * sub + 2].astype(jnp.float32) * 0.25
            b = params_ref[i_own, 4 * sub + 3].astype(jnp.float32) * 0.25
            row2 = lax.bitwise_and(row + 2 * side_row - 1, 3)
            base2 = jnp.where(side_col == parity, 0, 4)
            i_row = 8 + lax.bitwise_xor(lax.bitwise_xor(row2, grp), 2)
            i_col = base2 + lax.bitwise_xor(row, grp)
            i_diag = base2 + lax.bitwise_xor(row2, grp)
            terms = ((a * (1.0 - b), i_row), ((1.0 - a) * b, i_col), (a * b, i_diag))
            plans.append(((1.0 - a) * (1.0 - b), terms))

        @pl.loop(0, count // 16, unroll=2)
        def _(step):
            at = pl.ds(pl.multiple_of(step * 16, 16), 16)
            own_part = table[8 + i_own, at, :].astype(jnp.float32)
            for sub, (weight, terms) in enumerate(plans):
                mixed = weight * own_part
                for share, index in terms:
                    mixed = mixed + share * table[index, at, :].astype(jnp.float32)
                out_ref[4 * row + sub, at, :] = mixed.astype(jnp.bfloat16)


def blend_centres(where, params, own, side, cross0, cross123, first, count):
    smem = pl.BlockSpec(memory_space=pltpu.SMEM)
    return pl.pallas_call(
        functools.partial(blend_kernel, first, count),
        out_shape=jax.ShapeDtypeStruct((16, count, K), jnp.bfloat16),
        in_specs=[smem, smem] + [pl.BlockSpec(memory_space=pltpu.HBM)] * 4,
        out_specs=pl.BlockSpec(memory_space=pltpu.VMEM),
        scratch_shapes=[
            pltpu.VMEM((12, count, K), jnp.bfloat16),
            pltpu.SemaphoreType.DMA((4,)),
        ],
        compiler_params=pltpu.CompilerParams(vmem_limit_bytes=VMEM_LIMIT),
        cost_estimate=LIGHT,
    )(where, params, own, side, cross0, cross123)


def sub_block(product, cols, rows):
    lane = lax.broadcasted_iota(jnp.int32, (rows, 128), 1)
    return jnp.where(lane < 64, product[:rows, cols], product[rows:, cols])


def side_by_side(refs, half, row, at):
    return jnp.concatenate(
        [ref[:, half, pl.ds(row, 1), :, at].reshape(HALF, 128) for ref in refs], axis=1
    )


def here_kernel(blend_ref, mine, near, out_ref):
    count = blend_ref.shape[1]

    @pl.loop(0, 4, unroll=2)
    def _(row):
        for pair in range(2):
            at = slice(pair * 128, pair * 128 + 128)
            for two in range(2):
                half = 1 - two
                left = blend_ref[pl.ds(4 * row + 2 * pair, 2), :, half * HALF : half * HALF + HALF]
                product = jnp.dot(
                    left.reshape(2 * count, HALF),
                    side_by_side((mine, near), half, row, at),
                    preferred_element_type=jnp.float32,
                )
                for n in range(2):
                    out_ref[2 * pair + two, n, row] = sub_block(
                        product, slice(n * 128, n * 128 + 128), count
                    )


def apply_here(blend, mine, near):
    vmem = pl.BlockSpec(memory_space=pltpu.VMEM)
    return pl.pallas_call(
        here_kernel,
        out_shape=jax.ShapeDtypeStruct((4, 2, 4, blend.shape[1], 128), jnp.float32),
        in_specs=[vmem] * 3,
        out_specs=vmem,
        compiler_params=pltpu.CompilerParams(vmem_limit_bytes=VMEM_LIMIT),
        cost_estimate=LIGHT,
    )(blend, mine.reshape(32, 2, 4, 16, 256), near.reshape(32, 2, 4, 16, 256))


def apply_kernel(where_ref, blend_a, blend_b, part_a, part_b, far, far_near, out_ref, total):
    quarter = where_ref[2]
    rest = JQ - CUT

    @pl.loop(0, 4, unroll=2)
    def _(row):
        for pair in range(2):
            at = slice(pair * 128, pair * 128 + 128)
            subs = pl.ds(4 * row + 2 * pair, 2)
            for two in range(2):
                lanes = slice(two * HALF, two * HALF + HALF)
                left = jnp.concatenate(
                    [
                        blend_a[subs, :, lanes].reshape(2 * CUT, HALF),
                        blend_b[subs, :, lanes].reshape(2 * rest, HALF),
                    ],
                    axis=0,
                )
                product = jnp.dot(
                    left,
                    side_by_side((far, far_near), two, row, at),
                    preferred_element_type=jnp.float32,
                )
                for n in range(2):
                    cols = slice(n * 128, n * 128 + 128)
                    to = (pair, 2 * two + n)
                    total[(*to, pl.ds(row, CUT, stride=4), slice(None))] = (
                        sub_block(product[: 2 * CUT], cols, CUT) + part_a[2 * pair + two, n, row]
                    )
                    total[(*to, pl.ds(row + 4 * CUT, rest, stride=4), slice(None))] = (
                        sub_block(product[2 * CUT :], cols, rest) + part_b[2 * pair + two, n, row]
                    )

    for rho in range(4):
        level = lax.bitwise_xor(quarter, rho)
        for pair in range(2):
            at = slice(pair * 128, pair * 128 + 128)
            done = total[pair, rho].reshape(32, 2, 16, 128).astype(jnp.bfloat16)
            out_ref[lax.bitwise_xor(level, 2), :, 0, :, at] = done[:, 0]
            out_ref[level, :, 1, :, at] = done[:, 1]


def apply_transforms(where, blend_a, blend_b, part_a, part_b, fields):
    vmem = pl.BlockSpec(memory_space=pltpu.VMEM)
    return pl.pallas_call(
        apply_kernel,
        out_shape=jax.ShapeDtypeStruct((4, 32, 2, 16, 256), jnp.bfloat16),
        in_specs=[pl.BlockSpec(memory_space=pltpu.SMEM)] + [vmem] * 6,
        out_specs=vmem,
        scratch_shapes=[pltpu.VMEM((2, 4, 4 * JQ, 128), jnp.float32)],
        compiler_params=pltpu.CompilerParams(vmem_limit_bytes=VMEM_LIMIT),
        cost_estimate=LIGHT,
    )(where, blend_a, blend_b, part_a, part_b, *(f.reshape(32, 2, 4, 16, 256) for f in fields))


def body(fields, centres, sides, quarters):
    shift = functools.partial(lax.ppermute, axis_name=AX)
    grp = lax.axis_index("grp")
    parity = lax.bitwise_and(lax.axis_index("mem"), 1)
    where = jnp.stack([grp, parity, lax.bitwise_xor(grp, 2 * parity)]).astype(jnp.int32)

    by_col = with_layout_constraint(
        fields[0].transpose(2, 1, 0, 3), Layout(major_to_minor=(0, 1, 2, 3))
    )
    mine = lax.all_to_all(by_col, AX, 0, 0, axis_index_groups=FIELD_GROUPS, tiled=True)

    keep, to_mate, to_far = split_centres(where, sides[0, 0], quarters[0, 0], centres[0, 0])
    mate = shift(to_mate, perm=CORE)
    own23 = shift(jnp.stack([to_far, mate[1]]), perm=PAL)
    cross0 = shift(keep, perm=CROSS)
    own_a = jnp.concatenate([keep[None, :CUT], mate[:1, :CUT], own23[:, :CUT]])
    own_b = jnp.concatenate([keep[None, CUT:JQ], mate[:1, CUT:JQ], own23[:, CUT:JQ]])
    own123 = jnp.concatenate([mate[:1, :JQ], own23[:, :JQ]])
    params = jnp.concatenate([keep[None, JQ, :128], mate[:1, JQ, :128], own23[:, JQ, :128]])
    params = shift(params, perm=CROSS)
    mine, own123, own_a, own_b, cross0, params = lax.optimization_barrier(
        (mine, own123, own_a, own_b, cross0, params)
    )

    far = shift(mine, perm=PAL)
    side_a = shift(own_a, perm=SIDE)
    cross123 = shift(own123, perm=CROSS)
    side_b = shift(own_b, perm=SIDE)
    near = shift(mine, perm=CORE)
    params = params[:, :16].astype(jnp.int32)
    blend_a = blend_centres(where, params, own_a, side_a, cross0, cross123, 0, CUT)
    part_a = apply_here(blend_a, mine, near)
    far, part_a, side_b = lax.optimization_barrier((far, part_a, side_b))
    far_near = shift(far, perm=CORE)
    blend_b = blend_centres(where, params, own_b, side_b, cross0, cross123, CUT, JQ - CUT)
    part_b = apply_here(blend_b, mine, near)
    result = apply_transforms(where, blend_a, blend_b, part_a, part_b, (far, far_near))

    got = lax.all_to_all(
        result.reshape(MEM * GRP, 16, 256), AX, 0, 0, axis_index_groups=RESULT_GROUP, tiled=True
    )
    return got.reshape(GRP, MEM, 16, 256).transpose(0, 2, 1, 3).reshape(1, 16, 4, MEM, 256)


def solution(mesh):
    return jax.shard_map(
        body,
        mesh=mesh,
        in_specs=(
            P("grp", "mem", None, None, None),
            P("grp", "mem", None, None),
            P("grp", "mem", None, None),
            P("grp", "mem", None, None),
        ),
        out_specs=P("grp", "mem", None, None, None),
        check_vma=False,
    )
```

```python
import functools

import jax
import jax.numpy as jnp
from jax import lax
from jax.experimental import pallas as pl
from jax.experimental.layout import Layout, with_layout_constraint
from jax.experimental.pallas import tpu as pltpu
from jax.sharding import PartitionSpec as P

AX = ("mem", "grp")
MEM = 64
GRP = 4
K = 1024
JQ = 256
JP = JQ + 16
HALF = K // 2
CUT = 192


def flat_perm(move):
    pairs = []
    for mem in range(MEM):
        for grp in range(GRP):
            to_mem, to_grp = move(mem, grp)
            pairs.append((mem * GRP + grp, (to_mem % MEM) * GRP + to_grp))
    return pairs


CORE = flat_perm(lambda m, g: (m, g ^ 1))
PAL = flat_perm(lambda m, g: (m, g ^ 2))
CROSS = flat_perm(lambda m, g: (m ^ 1, g ^ 2))
SIDE = flat_perm(lambda m, g: (m + 2 if m % 2 else m - 2, g))


FIELD_GROUPS = [
    [(c ^ 1) * GRP + 2 * (((c ^ 1) & 1) ^ flank) + core for c in range(MEM)]
    for flank in range(2)
    for core in range(2)
]
RESULT_GROUP = [
    [(c ^ 1) * GRP + (quarter ^ (2 * ((c ^ 1) & 1))) for quarter in range(GRP) for c in range(MEM)]
]
VMEM_LIMIT = 24 * 1024 * 1024
LIGHT = pl.CostEstimate(flops=1, bytes_accessed=1, transcendentals=0)


def split_kernel(where_ref, sides_ref, quarters_ref, centre_ref, keep_ref, mate_ref, far_ref):
    grp = where_ref[0]
    parity = where_ref[1]
    row = lax.broadcasted_iota(jnp.int32, (JQ, K), 0)
    col = lax.broadcasted_iota(jnp.int32, (JQ, K), 1)
    base = lax.bitwise_xor(row // 4, 1) * 16 + row % 4
    lane = lax.broadcasted_iota(jnp.int32, (16, K), 1)
    small = jnp.zeros((16, K), jnp.int32)
    for sub in range(4):
        for n in range(2):
            small = jnp.where(lane == 4 * sub + n, sides_ref[sub, n], small)
            small = jnp.where(lane == 4 * sub + 2 + n, quarters_ref[sub, n], small)
    small = small.astype(jnp.float32).astype(jnp.bfloat16)
    ordered = jnp.concatenate(
        [centre_ref[:, 1].reshape(HALF, K), centre_ref[:, 0].reshape(HALF, K)], axis=0
    )
    for rho, out in enumerate((keep_ref, mate_ref.at[0], far_ref, mate_ref.at[1])):
        quarter = lax.bitwise_xor(lax.bitwise_xor(grp, rho), 2 * parity)
        pick = jnp.where(col == base + 4 * quarter, 1.0, 0.0).astype(jnp.bfloat16)
        out[:JQ, :] = lax.dot_general(
            pick, ordered, (((1,), (1,)), ((), ())), preferred_element_type=jnp.float32
        ).astype(jnp.bfloat16)
        out[JQ:, :] = small


def split_centres(where, sides, quarters, centre):
    smem = pl.BlockSpec(memory_space=pltpu.SMEM)
    vmem = pl.BlockSpec(memory_space=pltpu.VMEM)
    one = jax.ShapeDtypeStruct((JP, K), jnp.bfloat16)
    two = jax.ShapeDtypeStruct((2, JP, K), jnp.bfloat16)
    return pl.pallas_call(
        split_kernel,
        out_shape=[one, two, one],
        in_specs=[smem, smem, smem, vmem],
        out_specs=[vmem] * 3,
        compiler_params=pltpu.CompilerParams(vmem_limit_bytes=VMEM_LIMIT),
        cost_estimate=LIGHT,
    )(where, sides, quarters, centre.reshape(32, 2, 16, K))


def blend_kernel(first, count, where_ref, params_ref, cross0, cross123, own, side, out_ref, table, sems):
    grp = where_ref[0]
    parity = where_ref[1]
    at = pl.ds(first, count)
    ends = (
        (own, table.at[0:4]),
        (side, table.at[4:8]),
        (cross0.at[at], table.at[8]),
        (cross123.at[:, at], table.at[9:12]),
    )
    copies = [pltpu.make_async_copy(a, b, sems.at[n]) for n, (a, b) in enumerate(ends)]
    for copy in copies:
        copy.start()
    for copy in copies:
        copy.wait()

    @pl.loop(0, 4)
    def _(row):
        i_own = lax.bitwise_xor(lax.bitwise_xor(row, grp), 2)
        plans = []
        for sub in range(4):
            side_row = params_ref[i_own, 4 * sub]
            side_col = params_ref[i_own, 4 * sub + 1]
            a = params_ref[i_own, 4 * sub + 2].astype(jnp.float32) * 0.25
            b = params_ref[i_own, 4 * sub + 3].astype(jnp.float32) * 0.25
            row2 = lax.bitwise_and(row + 2 * side_row - 1, 3)
            base2 = jnp.where(side_col == parity, 0, 4)
            i_row = 8 + lax.bitwise_xor(lax.bitwise_xor(row2, grp), 2)
            i_col = base2 + lax.bitwise_xor(row, grp)
            i_diag = base2 + lax.bitwise_xor(row2, grp)
            terms = ((a * (1.0 - b), i_row), ((1.0 - a) * b, i_col), (a * b, i_diag))
            plans.append(((1.0 - a) * (1.0 - b), terms))

        @pl.loop(0, count // 16, unroll=2)
        def _(step):
            at = pl.ds(pl.multiple_of(step * 16, 16), 16)
            own_part = table[8 + i_own, at, :].astype(jnp.float32)
            for sub, (weight, terms) in enumerate(plans):
                mixed = weight * own_part
                for share, index in terms:
                    mixed = mixed + share * table[index, at, :].astype(jnp.float32)
                out_ref[4 * row + sub, at, :] = mixed.astype(jnp.bfloat16)


def blend_centres(where, params, own, side, cross0, cross123, first, count):
    smem = pl.BlockSpec(memory_space=pltpu.SMEM)
    return pl.pallas_call(
        functools.partial(blend_kernel, first, count),
        out_shape=jax.ShapeDtypeStruct((16, count, K), jnp.bfloat16),
        in_specs=[smem, smem] + [pl.BlockSpec(memory_space=pltpu.HBM)] * 4,
        out_specs=pl.BlockSpec(memory_space=pltpu.VMEM),
        scratch_shapes=[
            pltpu.VMEM((12, count, K), jnp.bfloat16),
            pltpu.SemaphoreType.DMA((4,)),
        ],
        compiler_params=pltpu.CompilerParams(vmem_limit_bytes=VMEM_LIMIT),
        cost_estimate=LIGHT,
    )(where, params, cross0, cross123, own, side)


def sub_block(product, cols, rows):
    lane = lax.broadcasted_iota(jnp.int32, (rows, 128), 1)
    return jnp.where(lane < 64, product[:rows, cols], product[rows:, cols])


def side_by_side(refs, half, row, at):
    return jnp.concatenate(
        [ref[:, half, pl.ds(row, 1), :, at].reshape(HALF, 128) for ref in refs], axis=1
    )


def here_kernel(blend_ref, mine, near, out_ref):
    count = blend_ref.shape[1]

    @pl.loop(0, 4, unroll=2)
    def _(row):
        for pair in range(2):
            at = slice(pair * 128, pair * 128 + 128)
            for two in range(2):
                half = 1 - two
                left = blend_ref[pl.ds(4 * row + 2 * pair, 2), :, half * HALF : half * HALF + HALF]
                product = jnp.dot(
                    left.reshape(2 * count, HALF),
                    side_by_side((mine, near), half, row, at),
                    preferred_element_type=jnp.float32,
                )
                for n in range(2):
                    out_ref[2 * pair + two, n, row] = sub_block(
                        product, slice(n * 128, n * 128 + 128), count
                    )


def apply_here(blend, mine, near):
    vmem = pl.BlockSpec(memory_space=pltpu.VMEM)
    return pl.pallas_call(
        here_kernel,
        out_shape=jax.ShapeDtypeStruct((4, 2, 4, blend.shape[1], 128), jnp.float32),
        in_specs=[vmem] * 3,
        out_specs=vmem,
        compiler_params=pltpu.CompilerParams(vmem_limit_bytes=VMEM_LIMIT),
        cost_estimate=LIGHT,
    )(blend, mine.reshape(32, 2, 4, 16, 256), near.reshape(32, 2, 4, 16, 256))


def apply_kernel(where_ref, blend_a, blend_b, part_a, part_b, far, far_near, out_ref, total):
    quarter = where_ref[2]
    rest = JQ - CUT

    @pl.loop(0, 4, unroll=2)
    def _(row):
        for pair in range(2):
            at = slice(pair * 128, pair * 128 + 128)
            subs = pl.ds(4 * row + 2 * pair, 2)
            for two in range(2):
                lanes = slice(two * HALF, two * HALF + HALF)
                left = jnp.concatenate(
                    [
                        blend_a[subs, :, lanes].reshape(2 * CUT, HALF),
                        blend_b[subs, :, lanes].reshape(2 * rest, HALF),
                    ],
                    axis=0,
                )
                product = jnp.dot(
                    left,
                    side_by_side((far, far_near), two, row, at),
                    preferred_element_type=jnp.float32,
                )
                for n in range(2):
                    cols = slice(n * 128, n * 128 + 128)
                    to = (pair, 2 * two + n)
                    total[(*to, pl.ds(row, CUT, stride=4), slice(None))] = (
                        sub_block(product[: 2 * CUT], cols, CUT) + part_a[2 * pair + two, n, row]
                    )
                    total[(*to, pl.ds(row + 4 * CUT, rest, stride=4), slice(None))] = (
                        sub_block(product[2 * CUT :], cols, rest) + part_b[2 * pair + two, n, row]
                    )

    for rho in range(4):
        level = lax.bitwise_xor(quarter, rho)
        for pair in range(2):
            at = slice(pair * 128, pair * 128 + 128)
            done = total[pair, rho, : 4 * JQ].reshape(32, 2, 16, 128).astype(jnp.bfloat16)
            out_ref[lax.bitwise_xor(level, 2), :, 0, :, at] = done[:, 0]
            out_ref[level, :, 1, :, at] = done[:, 1]


def apply_transforms(where, blend_a, blend_b, part_a, part_b, fields):
    vmem = pl.BlockSpec(memory_space=pltpu.VMEM)
    return pl.pallas_call(
        apply_kernel,
        out_shape=jax.ShapeDtypeStruct((4, 32, 2, 16, 256), jnp.bfloat16),
        in_specs=[pl.BlockSpec(memory_space=pltpu.SMEM)] + [vmem] * 6,
        out_specs=vmem,
        scratch_shapes=[pltpu.VMEM((2, 4, 4 * JQ + 8, 128), jnp.float32)],
        compiler_params=pltpu.CompilerParams(vmem_limit_bytes=VMEM_LIMIT),
        cost_estimate=LIGHT,
    )(where, blend_a, blend_b, part_a, part_b, *(f.reshape(32, 2, 4, 16, 256) for f in fields))


def body(fields, centres, sides, quarters):
    shift = functools.partial(lax.ppermute, axis_name=AX)
    grp = lax.axis_index("grp")
    parity = lax.bitwise_and(lax.axis_index("mem"), 1)
    where = jnp.stack([grp, parity, lax.bitwise_xor(grp, 2 * parity)]).astype(jnp.int32)

    by_col = with_layout_constraint(
        fields[0].transpose(2, 1, 0, 3), Layout(major_to_minor=(0, 1, 2, 3))
    )
    mine = lax.all_to_all(by_col, AX, 0, 0, axis_index_groups=FIELD_GROUPS, tiled=True)

    keep, to_mate, to_far = split_centres(where, sides[0, 0], quarters[0, 0], centres[0, 0])
    mate = shift(to_mate, perm=CORE)
    own23 = shift(jnp.stack([to_far, mate[1]]), perm=PAL)
    cross0 = shift(keep, perm=CROSS)
    own_a = jnp.concatenate([keep[None, :CUT], mate[:1, :CUT], own23[:, :CUT]])
    own_b = jnp.concatenate([keep[None, CUT:JQ], mate[:1, CUT:JQ], own23[:, CUT:JQ]])
    own123 = jnp.concatenate([mate[:1, :JQ], own23[:, :JQ]])
    params = jnp.concatenate([keep[None, JQ, :128], mate[:1, JQ, :128], own23[:, JQ, :128]])
    params = shift(params, perm=CROSS)
    mine, own123, own_a, own_b, cross0, params = lax.optimization_barrier(
        (mine, own123, own_a, own_b, cross0, params)
    )

    far = shift(mine, perm=PAL)
    cross123 = shift(own123, perm=CROSS)
    side_a = shift(own_a, perm=SIDE)
    side_b = shift(own_b, perm=SIDE)
    near = shift(mine, perm=CORE)
    params = params[:, :16].astype(jnp.int32)
    blend_a = blend_centres(where, params, own_a, side_a, cross0, cross123, 0, CUT)
    part_a = apply_here(blend_a, mine, near)
    far, part_a, side_b = lax.optimization_barrier((far, part_a, side_b))
    far_near = shift(far, perm=CORE)
    blend_b = blend_centres(where, params, own_b, side_b, cross0, cross123, CUT, JQ - CUT)
    part_b = apply_here(blend_b, mine, near)
    result = apply_transforms(where, blend_a, blend_b, part_a, part_b, (far, far_near))

    got = lax.all_to_all(
        result.reshape(MEM * GRP, 16, 256), AX, 0, 0, axis_index_groups=RESULT_GROUP, tiled=True
    )
    return got.reshape(GRP, MEM, 16, 256).transpose(0, 2, 1, 3).reshape(1, 16, 4, MEM, 256)


def solution(mesh):
    return jax.shard_map(
        body,
        mesh=mesh,
        in_specs=(
            P("grp", "mem", None, None, None),
            P("grp", "mem", None, None),
            P("grp", "mem", None, None),
            P("grp", "mem", None, None),
        ),
        out_specs=P("grp", "mem", None, None, None),
        check_vma=False,
    )
```

```python
import functools

import jax
import jax.numpy as jnp
from jax import lax
from jax.experimental import pallas as pl
from jax.experimental.layout import Layout, with_layout_constraint
from jax.experimental.pallas import tpu as pltpu
from jax.sharding import PartitionSpec as P

AX = ("mem", "grp")
MEM = 64
GRP = 4
K = 1024
JQ = 256
JP = JQ + 16
HALF = K // 2
CUT = 192


def flat_perm(move):
    pairs = []
    for mem in range(MEM):
        for grp in range(GRP):
            to_mem, to_grp = move(mem, grp)
            pairs.append((mem * GRP + grp, (to_mem % MEM) * GRP + to_grp))
    return pairs


CORE = flat_perm(lambda m, g: (m, g ^ 1))
PAL = flat_perm(lambda m, g: (m, g ^ 2))
CROSS = flat_perm(lambda m, g: (m ^ 1, g ^ 2))
SIDE = flat_perm(lambda m, g: (m + 2 if m % 2 else m - 2, g))


def way_round(last):
    def move(m, g):
        z, x, parity = m // 8, m // 2 % 4, m % 2
        if parity:
            to_z, to_x = z + (last and x == 1), (x - 1) % 4
        else:
            to_z, to_x = z - (last and x == 2), (x + 1) % 4
        return to_z % 8 * 8 + to_x * 2 + parity, g

    return flat_perm(move)


BACK = way_round(False)
BACK_END = way_round(True)
FIELD_GROUPS = [
    [(c ^ 1) * GRP + 2 * (((c ^ 1) & 1) ^ flank) + core for c in range(MEM)]
    for flank in range(2)
    for core in range(2)
]
RESULT_GROUP = [
    [(c ^ 1) * GRP + (quarter ^ (2 * ((c ^ 1) & 1))) for quarter in range(GRP) for c in range(MEM)]
]
VMEM_LIMIT = 24 * 1024 * 1024
LIGHT = pl.CostEstimate(flops=1, bytes_accessed=1, transcendentals=0)


def split_kernel(where_ref, sides_ref, quarters_ref, centre_ref, keep_ref, mate_ref, far_ref):
    grp = where_ref[0]
    parity = where_ref[1]
    row = lax.broadcasted_iota(jnp.int32, (JQ, K), 0)
    col = lax.broadcasted_iota(jnp.int32, (JQ, K), 1)
    base = lax.bitwise_xor(row // 4, 1) * 16 + row % 4
    lane = lax.broadcasted_iota(jnp.int32, (16, K), 1)
    small = jnp.zeros((16, K), jnp.int32)
    for sub in range(4):
        for n in range(2):
            small = jnp.where(lane == 4 * sub + n, sides_ref[sub, n], small)
            small = jnp.where(lane == 4 * sub + 2 + n, quarters_ref[sub, n], small)
    small = small.astype(jnp.float32).astype(jnp.bfloat16)
    ordered = jnp.concatenate(
        [centre_ref[:, 1].reshape(HALF, K), centre_ref[:, 0].reshape(HALF, K)], axis=0
    )
    for rho, out in enumerate((keep_ref, mate_ref.at[0], far_ref, mate_ref.at[1])):
        quarter = lax.bitwise_xor(lax.bitwise_xor(grp, rho), 2 * parity)
        pick = jnp.where(col == base + 4 * quarter, 1.0, 0.0).astype(jnp.bfloat16)
        out[:JQ, :] = lax.dot_general(
            pick, ordered, (((1,), (1,)), ((), ())), preferred_element_type=jnp.float32
        ).astype(jnp.bfloat16)
        out[JQ:, :] = small


def split_centres(where, sides, quarters, centre):
    smem = pl.BlockSpec(memory_space=pltpu.SMEM)
    vmem = pl.BlockSpec(memory_space=pltpu.VMEM)
    one = jax.ShapeDtypeStruct((JP, K), jnp.bfloat16)
    two = jax.ShapeDtypeStruct((2, JP, K), jnp.bfloat16)
    return pl.pallas_call(
        split_kernel,
        out_shape=[one, two, one],
        in_specs=[smem, smem, smem, vmem],
        out_specs=[vmem] * 3,
        compiler_params=pltpu.CompilerParams(vmem_limit_bytes=VMEM_LIMIT),
        cost_estimate=LIGHT,
    )(where, sides, quarters, centre.reshape(32, 2, 16, K))


def blend_kernel(first, count, where_ref, params_ref, cross0, cross123, own, side, out_ref, table, sems):
    grp = where_ref[0]
    parity = where_ref[1]
    at = pl.ds(first, count)
    ends = (
        (own, table.at[0:4]),
        (side, table.at[4:8]),
        (cross0.at[at], table.at[8]),
        (cross123.at[:, at], table.at[9:12]),
    )
    copies = [pltpu.make_async_copy(a, b, sems.at[n]) for n, (a, b) in enumerate(ends)]
    for copy in copies:
        copy.start()
    for copy in copies:
        copy.wait()

    @pl.loop(0, 4)
    def _(row):
        i_own = lax.bitwise_xor(lax.bitwise_xor(row, grp), 2)
        plans = []
        for sub in range(4):
            side_row = params_ref[i_own, 4 * sub]
            side_col = params_ref[i_own, 4 * sub + 1]
            a = params_ref[i_own, 4 * sub + 2].astype(jnp.float32) * 0.25
            b = params_ref[i_own, 4 * sub + 3].astype(jnp.float32) * 0.25
            row2 = lax.bitwise_and(row + 2 * side_row - 1, 3)
            base2 = jnp.where(side_col == parity, 0, 4)
            i_row = 8 + lax.bitwise_xor(lax.bitwise_xor(row2, grp), 2)
            i_col = base2 + lax.bitwise_xor(row, grp)
            i_diag = base2 + lax.bitwise_xor(row2, grp)
            terms = ((a * (1.0 - b), i_row), ((1.0 - a) * b, i_col), (a * b, i_diag))
            plans.append(((1.0 - a) * (1.0 - b), terms))

        @pl.loop(0, count // 16, unroll=2)
        def _(step):
            at = pl.ds(pl.multiple_of(step * 16, 16), 16)
            own_part = table[8 + i_own, at, :].astype(jnp.float32)
            for sub, (weight, terms) in enumerate(plans):
                mixed = weight * own_part
                for share, index in terms:
                    mixed = mixed + share * table[index, at, :].astype(jnp.float32)
                out_ref[4 * row + sub, at, :] = mixed.astype(jnp.bfloat16)


def blend_centres(where, params, own, side, cross0, cross123, first, count):
    smem = pl.BlockSpec(memory_space=pltpu.SMEM)
    return pl.pallas_call(
        functools.partial(blend_kernel, first, count),
        out_shape=jax.ShapeDtypeStruct((16, count, K), jnp.bfloat16),
        in_specs=[smem, smem] + [pl.BlockSpec(memory_space=pltpu.HBM)] * 4,
        out_specs=pl.BlockSpec(memory_space=pltpu.VMEM),
        scratch_shapes=[
            pltpu.VMEM((12, count, K), jnp.bfloat16),
            pltpu.SemaphoreType.DMA((4,)),
        ],
        compiler_params=pltpu.CompilerParams(vmem_limit_bytes=VMEM_LIMIT),
        cost_estimate=LIGHT,
    )(where, params, cross0, cross123, own, side)


def sub_block(product, cols, rows):
    lane = lax.broadcasted_iota(jnp.int32, (rows, 128), 1)
    return jnp.where(lane < 64, product[:rows, cols], product[rows:, cols])


def side_by_side(refs, half, row, at):
    return jnp.concatenate(
        [ref[:, half, pl.ds(row, 1), :, at].reshape(HALF, 128) for ref in refs], axis=1
    )


def here_kernel(blend_ref, mine, near, out_ref):
    count = blend_ref.shape[1]

    @pl.loop(0, 4, unroll=2)
    def _(row):
        for pair in range(2):
            at = slice(pair * 128, pair * 128 + 128)
            for two in range(2):
                half = 1 - two
                left = blend_ref[pl.ds(4 * row + 2 * pair, 2), :, half * HALF : half * HALF + HALF]
                product = jnp.dot(
                    left.reshape(2 * count, HALF),
                    side_by_side((mine, near), half, row, at),
                    preferred_element_type=jnp.float32,
                )
                for n in range(2):
                    out_ref[2 * pair + two, n, row] = sub_block(
                        product, slice(n * 128, n * 128 + 128), count
                    )


def apply_here(blend, mine, near):
    vmem = pl.BlockSpec(memory_space=pltpu.VMEM)
    return pl.pallas_call(
        here_kernel,
        out_shape=jax.ShapeDtypeStruct((4, 2, 4, blend.shape[1], 128), jnp.float32),
        in_specs=[vmem] * 3,
        out_specs=vmem,
        compiler_params=pltpu.CompilerParams(vmem_limit_bytes=VMEM_LIMIT),
        cost_estimate=LIGHT,
    )(blend, mine.reshape(32, 2, 4, 16, 256), near.reshape(32, 2, 4, 16, 256))


def apply_kernel(where_ref, blend_a, blend_b, part_a, part_b, far, far_near, out_ref, total):
    quarter = where_ref[2]
    rest = JQ - CUT

    @pl.loop(0, 4, unroll=2)
    def _(row):
        for pair in range(2):
            at = slice(pair * 128, pair * 128 + 128)
            subs = pl.ds(4 * row + 2 * pair, 2)
            for two in range(2):
                lanes = slice(two * HALF, two * HALF + HALF)
                left = jnp.concatenate(
                    [
                        blend_a[subs, :, lanes].reshape(2 * CUT, HALF),
                        blend_b[subs, :, lanes].reshape(2 * rest, HALF),
                    ],
                    axis=0,
                )
                product = jnp.dot(
                    left,
                    side_by_side((far, far_near), two, row, at),
                    preferred_element_type=jnp.float32,
                )
                for n in range(2):
                    cols = slice(n * 128, n * 128 + 128)
                    to = (pair, 2 * two + n)
                    total[(*to, pl.ds(row, CUT, stride=4), slice(None))] = (
                        sub_block(product[: 2 * CUT], cols, CUT) + part_a[2 * pair + two, n, row]
                    )
                    total[(*to, pl.ds(row + 4 * CUT, rest, stride=4), slice(None))] = (
                        sub_block(product[2 * CUT :], cols, rest) + part_b[2 * pair + two, n, row]
                    )

    for rho in range(4):
        level = lax.bitwise_xor(quarter, rho)
        for pair in range(2):
            at = slice(pair * 128, pair * 128 + 128)
            done = total[pair, rho, : 4 * JQ].reshape(32, 2, 16, 128).astype(jnp.bfloat16)
            out_ref[lax.bitwise_xor(level, 2), :, 0, :, at] = done[:, 0]
            out_ref[level, :, 1, :, at] = done[:, 1]


def apply_transforms(where, blend_a, blend_b, part_a, part_b, fields):
    vmem = pl.BlockSpec(memory_space=pltpu.VMEM)
    return pl.pallas_call(
        apply_kernel,
        out_shape=jax.ShapeDtypeStruct((4, 32, 2, 16, 256), jnp.bfloat16),
        in_specs=[pl.BlockSpec(memory_space=pltpu.SMEM)] + [vmem] * 6,
        out_specs=vmem,
        scratch_shapes=[pltpu.VMEM((2, 4, 4 * JQ + 8, 128), jnp.float32)],
        compiler_params=pltpu.CompilerParams(vmem_limit_bytes=VMEM_LIMIT),
        cost_estimate=LIGHT,
    )(where, blend_a, blend_b, part_a, part_b, *(f.reshape(32, 2, 4, 16, 256) for f in fields))


def body(fields, centres, sides, quarters):
    shift = functools.partial(lax.ppermute, axis_name=AX)
    grp = lax.axis_index("grp")
    parity = lax.bitwise_and(lax.axis_index("mem"), 1)
    where = jnp.stack([grp, parity, lax.bitwise_xor(grp, 2 * parity)]).astype(jnp.int32)

    by_col = with_layout_constraint(
        fields[0].transpose(2, 1, 0, 3), Layout(major_to_minor=(0, 1, 2, 3))
    )
    mine = lax.all_to_all(by_col, AX, 0, 0, axis_index_groups=FIELD_GROUPS, tiled=True)

    keep, to_mate, to_far = split_centres(where, sides[0, 0], quarters[0, 0], centres[0, 0])
    mate = shift(to_mate, perm=CORE)
    own23 = shift(jnp.stack([to_far, mate[1]]), perm=PAL)
    cross0 = shift(keep, perm=CROSS)
    own_a = jnp.concatenate([keep[None, :CUT], mate[:1, :CUT], own23[:, :CUT]])
    own_b = jnp.concatenate([keep[None, CUT:JQ], mate[:1, CUT:JQ], own23[:, CUT:JQ]])
    own123 = jnp.concatenate([mate[:1, :JQ], own23[:, :JQ]])
    params = jnp.concatenate([keep[None, JQ, :128], mate[:1, JQ, :128], own23[:, JQ, :128]])
    params = shift(params, perm=CROSS)
    mine, own123, own_a, own_b, cross0, params = lax.optimization_barrier(
        (mine, own123, own_a, own_b, cross0, params)
    )

    far = shift(mine, perm=PAL)
    cross123 = shift(own123, perm=CROSS)
    side_a = shift(own_a, perm=SIDE)
    side_b = shift(shift(shift(own_b, perm=BACK), perm=BACK), perm=BACK_END)
    near = shift(mine, perm=CORE)
    params = params[:, :16].astype(jnp.int32)
    own_far = pltpu.with_memory_space_constraint(own_a, pltpu.HBM)
    blend_a = blend_centres(where, params, own_far, side_a, cross0, cross123, 0, CUT)
    part_a = apply_here(blend_a, mine, near)
    far, part_a, side_b = lax.optimization_barrier((far, part_a, side_b))
    far_near = shift(far, perm=CORE)
    blend_b = blend_centres(where, params, own_b, side_b, cross0, cross123, CUT, JQ - CUT)
    part_b = apply_here(blend_b, mine, near)
    result = apply_transforms(where, blend_a, blend_b, part_a, part_b, (far, far_near))

    got = lax.all_to_all(
        result.reshape(MEM * GRP, 16, 256), AX, 0, 0, axis_index_groups=RESULT_GROUP, tiled=True
    )
    return got.reshape(GRP, MEM, 16, 256).transpose(0, 2, 1, 3).reshape(1, 16, 4, MEM, 256)


def solution(mesh):
    return jax.shard_map(
        body,
        mesh=mesh,
        in_specs=(
            P("grp", "mem", None, None, None),
            P("grp", "mem", None, None),
            P("grp", "mem", None, None),
            P("grp", "mem", None, None),
        ),
        out_specs=P("grp", "mem", None, None, None),
        check_vma=False,
    )
```

```python
import functools

import jax
import jax.numpy as jnp
from jax import lax
from jax.experimental import pallas as pl
from jax.experimental.layout import Layout, with_layout_constraint
from jax.experimental.pallas import tpu as pltpu
from jax.sharding import PartitionSpec as P

AX = ("mem", "grp")
MEM = 64
GRP = 4
K = 1024
JQ = 256
JP = JQ + 16
HALF = K // 2
CUT = 192


def flat_perm(move):
    pairs = []
    for mem in range(MEM):
        for grp in range(GRP):
            to_mem, to_grp = move(mem, grp)
            pairs.append((mem * GRP + grp, (to_mem % MEM) * GRP + to_grp))
    return pairs


CORE = flat_perm(lambda m, g: (m, g ^ 1))
PAL = flat_perm(lambda m, g: (m, g ^ 2))
CROSS = flat_perm(lambda m, g: (m ^ 1, g ^ 2))
SIDE = flat_perm(lambda m, g: (m + 2 if m % 2 else m - 2, g))


def way_round(last):
    def move(m, g):
        z, x, parity = m // 8, m // 2 % 4, m % 2
        if parity:
            to_z, to_x = z + (last and x == 1), (x - 1) % 4
        else:
            to_z, to_x = z - (last and x == 2), (x + 1) % 4
        return to_z % 8 * 8 + to_x * 2 + parity, g

    return flat_perm(move)


BACK = way_round(False)
BACK_END = way_round(True)
FIELD_GROUPS = [
    [(c ^ 1) * GRP + 2 * (((c ^ 1) & 1) ^ flank) + core for c in range(MEM)]
    for flank in range(2)
    for core in range(2)
]
RESULT_GROUP = [
    [(c ^ 1) * GRP + (quarter ^ (2 * ((c ^ 1) & 1))) for quarter in range(GRP) for c in range(MEM)]
]
VMEM_LIMIT = 24 * 1024 * 1024
LIGHT = pl.CostEstimate(flops=1, bytes_accessed=1, transcendentals=0)


def split_kernel(where_ref, sides_ref, quarters_ref, centre_ref, keep_ref, mate_ref, far_ref):
    grp = where_ref[0]
    parity = where_ref[1]
    row = lax.broadcasted_iota(jnp.int32, (JQ, K), 0)
    col = lax.broadcasted_iota(jnp.int32, (JQ, K), 1)
    base = lax.bitwise_xor(row // 4, 1) * 16 + row % 4
    lane = lax.broadcasted_iota(jnp.int32, (16, K), 1)
    small = jnp.zeros((16, K), jnp.int32)
    for sub in range(4):
        for n in range(2):
            small = jnp.where(lane == 4 * sub + n, sides_ref[sub, n], small)
            small = jnp.where(lane == 4 * sub + 2 + n, quarters_ref[sub, n], small)
    small = small.astype(jnp.float32).astype(jnp.bfloat16)
    ordered = jnp.concatenate(
        [centre_ref[:, 1].reshape(HALF, K), centre_ref[:, 0].reshape(HALF, K)], axis=0
    )
    for rho, out in enumerate((keep_ref, mate_ref.at[0], far_ref, mate_ref.at[1])):
        quarter = lax.bitwise_xor(lax.bitwise_xor(grp, rho), 2 * parity)
        pick = jnp.where(col == base + 4 * quarter, 1.0, 0.0).astype(jnp.bfloat16)
        out[:JQ, :] = lax.dot_general(
            pick, ordered, (((1,), (1,)), ((), ())), preferred_element_type=jnp.float32
        ).astype(jnp.bfloat16)
        out[JQ:, :] = small


def split_centres(where, sides, quarters, centre):
    smem = pl.BlockSpec(memory_space=pltpu.SMEM)
    vmem = pl.BlockSpec(memory_space=pltpu.VMEM)
    one = jax.ShapeDtypeStruct((JP, K), jnp.bfloat16)
    two = jax.ShapeDtypeStruct((2, JP, K), jnp.bfloat16)
    return pl.pallas_call(
        split_kernel,
        out_shape=[one, two, one],
        in_specs=[smem, smem, smem, vmem],
        out_specs=[vmem] * 3,
        compiler_params=pltpu.CompilerParams(vmem_limit_bytes=VMEM_LIMIT),
        cost_estimate=LIGHT,
    )(where, sides, quarters, centre.reshape(32, 2, 16, K))


def blend_kernel(first, count, where_ref, params_ref, cross0, cross123, own, side, out_ref, table, sems):
    grp = where_ref[0]
    parity = where_ref[1]
    at = pl.ds(first, count)
    ends = (
        (own, table.at[0:4]),
        (side, table.at[4:8]),
        (cross0.at[at], table.at[8]),
        (cross123.at[:, at], table.at[9:12]),
    )
    copies = [pltpu.make_async_copy(a, b, sems.at[n]) for n, (a, b) in enumerate(ends)]
    for copy in copies:
        copy.start()
    for copy in copies:
        copy.wait()

    @pl.loop(0, 4)
    def _(row):
        i_own = lax.bitwise_xor(lax.bitwise_xor(row, grp), 2)
        plans = []
        for sub in range(4):
            side_row = params_ref[i_own, 4 * sub]
            side_col = params_ref[i_own, 4 * sub + 1]
            a = params_ref[i_own, 4 * sub + 2].astype(jnp.float32) * 0.25
            b = params_ref[i_own, 4 * sub + 3].astype(jnp.float32) * 0.25
            row2 = lax.bitwise_and(row + 2 * side_row - 1, 3)
            base2 = jnp.where(side_col == parity, 0, 4)
            i_row = 8 + lax.bitwise_xor(lax.bitwise_xor(row2, grp), 2)
            i_col = base2 + lax.bitwise_xor(row, grp)
            i_diag = base2 + lax.bitwise_xor(row2, grp)
            terms = ((a * (1.0 - b), i_row), ((1.0 - a) * b, i_col), (a * b, i_diag))
            plans.append(((1.0 - a) * (1.0 - b), terms))

        @pl.loop(0, count // 16, unroll=2)
        def _(step):
            at = pl.ds(pl.multiple_of(step * 16, 16), 16)
            own_part = table[8 + i_own, at, :].astype(jnp.float32)
            for sub, (weight, terms) in enumerate(plans):
                mixed = weight * own_part
                for share, index in terms:
                    mixed = mixed + share * table[index, at, :].astype(jnp.float32)
                out_ref[4 * row + sub, at, :] = mixed.astype(jnp.bfloat16)


def blend_centres(where, params, own, side, cross0, cross123, first, count):
    smem = pl.BlockSpec(memory_space=pltpu.SMEM)
    return pl.pallas_call(
        functools.partial(blend_kernel, first, count),
        out_shape=jax.ShapeDtypeStruct((16, count, K), jnp.bfloat16),
        in_specs=[smem, smem] + [pl.BlockSpec(memory_space=pltpu.HBM)] * 4,
        out_specs=pl.BlockSpec(memory_space=pltpu.VMEM),
        scratch_shapes=[
            pltpu.VMEM((12, count, K), jnp.bfloat16),
            pltpu.SemaphoreType.DMA((4,)),
        ],
        compiler_params=pltpu.CompilerParams(vmem_limit_bytes=VMEM_LIMIT),
        cost_estimate=LIGHT,
    )(where, params, cross0, cross123, own, side)


def sub_block(product, cols, rows):
    lane = lax.broadcasted_iota(jnp.int32, (rows, 128), 1)
    return jnp.where(lane < 64, product[:rows, cols], product[rows:, cols])


def side_by_side(refs, half, row, at):
    return jnp.concatenate(
        [ref[:, half, pl.ds(row, 1), :, at].reshape(HALF, 128) for ref in refs], axis=1
    )


def here_kernel(blend_ref, mine, near, out_ref):
    count = blend_ref.shape[1]

    @pl.loop(0, 4, unroll=2)
    def _(row):
        for pair in range(2):
            at = slice(pair * 128, pair * 128 + 128)
            for two in range(2):
                half = 1 - two
                left = blend_ref[pl.ds(4 * row + 2 * pair, 2), :, half * HALF : half * HALF + HALF]
                product = jnp.dot(
                    left.reshape(2 * count, HALF),
                    side_by_side((mine, near), half, row, at),
                    preferred_element_type=jnp.float32,
                )
                for n in range(2):
                    out_ref[2 * pair + two, n, row] = sub_block(
                        product, slice(n * 128, n * 128 + 128), count
                    )


def apply_here(blend, mine, near):
    vmem = pl.BlockSpec(memory_space=pltpu.VMEM)
    return pl.pallas_call(
        here_kernel,
        out_shape=jax.ShapeDtypeStruct((4, 2, 4, blend.shape[1], 128), jnp.float32),
        in_specs=[vmem] * 3,
        out_specs=vmem,
        compiler_params=pltpu.CompilerParams(vmem_limit_bytes=VMEM_LIMIT),
        cost_estimate=LIGHT,
    )(blend, mine.reshape(32, 2, 4, 16, 256), near.reshape(32, 2, 4, 16, 256))


def apply_kernel(where_ref, blend_a, blend_b, part_a, part_b, far, far_near, out_ref, total):
    quarter = where_ref[2]
    rest = JQ - CUT

    @pl.loop(0, 4, unroll=2)
    def _(row):
        for pair in range(2):
            at = slice(pair * 128, pair * 128 + 128)
            subs = pl.ds(4 * row + 2 * pair, 2)
            for two in range(2):
                lanes = slice(two * HALF, two * HALF + HALF)
                left = jnp.concatenate(
                    [
                        blend_a[subs, :, lanes].reshape(2 * CUT, HALF),
                        blend_b[subs, :, lanes].reshape(2 * rest, HALF),
                    ],
                    axis=0,
                )
                product = jnp.dot(
                    left,
                    side_by_side((far, far_near), two, row, at),
                    preferred_element_type=jnp.float32,
                )
                for n in range(2):
                    cols = slice(n * 128, n * 128 + 128)
                    to = (pair, 2 * two + n)
                    total[(*to, pl.ds(row, CUT, stride=4), slice(None))] = (
                        sub_block(product[: 2 * CUT], cols, CUT) + part_a[2 * pair + two, n, row]
                    )
                    total[(*to, pl.ds(row + 4 * CUT, rest, stride=4), slice(None))] = (
                        sub_block(product[2 * CUT :], cols, rest) + part_b[2 * pair + two, n, row]
                    )

    for rho in range(4):
        level = lax.bitwise_xor(quarter, rho)
        for pair in range(2):
            at = slice(pair * 128, pair * 128 + 128)
            done = total[pair, rho, : 4 * JQ].reshape(32, 2, 16, 128).astype(jnp.bfloat16)
            out_ref[lax.bitwise_xor(level, 2), :, 0, :, at] = done[:, 0]
            out_ref[level, :, 1, :, at] = done[:, 1]


def apply_transforms(where, blend_a, blend_b, part_a, part_b, fields):
    vmem = pl.BlockSpec(memory_space=pltpu.VMEM)
    return pl.pallas_call(
        apply_kernel,
        out_shape=jax.ShapeDtypeStruct((4, 32, 2, 16, 256), jnp.bfloat16),
        in_specs=[pl.BlockSpec(memory_space=pltpu.SMEM)] + [vmem] * 6,
        out_specs=vmem,
        scratch_shapes=[pltpu.VMEM((2, 4, 4 * JQ + 8, 128), jnp.float32)],
        compiler_params=pltpu.CompilerParams(vmem_limit_bytes=VMEM_LIMIT),
        cost_estimate=LIGHT,
    )(where, blend_a, blend_b, part_a, part_b, *(f.reshape(32, 2, 4, 16, 256) for f in fields))


def body(fields, centres, sides, quarters):
    shift = functools.partial(lax.ppermute, axis_name=AX)
    grp = lax.axis_index("grp")
    parity = lax.bitwise_and(lax.axis_index("mem"), 1)
    where = jnp.stack([grp, parity, lax.bitwise_xor(grp, 2 * parity)]).astype(jnp.int32)

    by_col = with_layout_constraint(
        fields[0].transpose(2, 1, 0, 3), Layout(major_to_minor=(0, 1, 2, 3))
    )
    mine = lax.all_to_all(by_col, AX, 0, 0, axis_index_groups=FIELD_GROUPS, tiled=True)

    keep, to_mate, to_far = split_centres(where, sides[0, 0], quarters[0, 0], centres[0, 0])
    mate = shift(to_mate, perm=CORE)
    own23 = shift(jnp.stack([to_far, mate[1]]), perm=PAL)
    cross0 = shift(keep, perm=CROSS)
    own_a = jnp.concatenate([keep[None, :CUT], mate[:1, :CUT], own23[:, :CUT]])
    own_b = jnp.concatenate([keep[None, CUT:JQ], mate[:1, CUT:JQ], own23[:, CUT:JQ]])
    own123 = jnp.concatenate([mate[:1, :JQ], own23[:, :JQ]])
    params = jnp.concatenate([keep[None, JQ, :128], mate[:1, JQ, :128], own23[:, JQ, :128]])
    params = shift(params, perm=CROSS)
    mine, own123, own_a, own_b, cross0, params = lax.optimization_barrier(
        (mine, own123, own_a, own_b, cross0, params)
    )

    far = shift(mine, perm=PAL)
    cross123 = shift(own123, perm=CROSS)
    side_a = shift(own_a, perm=SIDE)
    side_b = shift(shift(shift(own_b, perm=BACK), perm=BACK), perm=BACK_END)
    near = shift(mine, perm=CORE)
    params = params[:, :16].astype(jnp.int32)
    own_far = pltpu.with_memory_space_constraint(own_a, pltpu.HBM)
    blend_a = blend_centres(where, params, own_far, side_a, cross0, cross123, 0, CUT)
    far, blend_a, side_b = lax.optimization_barrier((far, blend_a, side_b))
    far_near = shift(far, perm=CORE)
    part_a = apply_here(blend_a, mine, near)
    blend_b = blend_centres(where, params, own_b, side_b, cross0, cross123, CUT, JQ - CUT)
    part_b = apply_here(blend_b, mine, near)
    result = apply_transforms(where, blend_a, blend_b, part_a, part_b, (far, far_near))

    got = lax.all_to_all(
        result.reshape(MEM * GRP, 16, 256), AX, 0, 0, axis_index_groups=RESULT_GROUP, tiled=True
    )
    return got.reshape(GRP, MEM, 16, 256).transpose(0, 2, 1, 3).reshape(1, 16, 4, MEM, 256)


def solution(mesh):
    return jax.shard_map(
        body,
        mesh=mesh,
        in_specs=(
            P("grp", "mem", None, None, None),
            P("grp", "mem", None, None),
            P("grp", "mem", None, None),
            P("grp", "mem", None, None),
        ),
        out_specs=P("grp", "mem", None, None, None),
        check_vma=False,
    )
```

```python
import functools

import jax
import jax.numpy as jnp
from jax import lax
from jax.experimental import pallas as pl
from jax.experimental.layout import Layout, with_layout_constraint
from jax.experimental.pallas import tpu as pltpu
from jax.sharding import PartitionSpec as P

AX = ("mem", "grp")
MEM = 64
GRP = 4
K = 1024
JQ = 256
JP = JQ + 16
HALF = K // 2
CUT = 192


def flat_perm(move):
    pairs = []
    for mem in range(MEM):
        for grp in range(GRP):
            to_mem, to_grp = move(mem, grp)
            pairs.append((mem * GRP + grp, (to_mem % MEM) * GRP + to_grp))
    return pairs


CORE = flat_perm(lambda m, g: (m, g ^ 1))
PAL = flat_perm(lambda m, g: (m, g ^ 2))
CROSS = flat_perm(lambda m, g: (m ^ 1, g ^ 2))
SIDE = flat_perm(lambda m, g: (m + 2 if m % 2 else m - 2, g))


def way_round(last):
    def move(m, g):
        z, x, parity = m // 8, m // 2 % 4, m % 2
        if parity:
            to_z, to_x = z + (last and x == 1), (x - 1) % 4
        else:
            to_z, to_x = z - (last and x == 2), (x + 1) % 4
        return to_z % 8 * 8 + to_x * 2 + parity, g

    return flat_perm(move)


BACK = way_round(False)
BACK_END = way_round(True)
FIELD_GROUPS = [
    [(c ^ 1) * GRP + 2 * (((c ^ 1) & 1) ^ flank) + core for c in range(MEM)]
    for flank in range(2)
    for core in range(2)
]
RESULT_GROUP = [
    [(c ^ 1) * GRP + (quarter ^ (2 * ((c ^ 1) & 1))) for quarter in range(GRP) for c in range(MEM)]
]
VMEM_LIMIT = 24 * 1024 * 1024
LIGHT = pl.CostEstimate(flops=1, bytes_accessed=1, transcendentals=0)


def split_kernel(where_ref, sides_ref, quarters_ref, centre_ref, keep_ref, mate_ref, far_ref):
    grp = where_ref[0]
    parity = where_ref[1]
    row = lax.broadcasted_iota(jnp.int32, (JQ, K), 0)
    col = lax.broadcasted_iota(jnp.int32, (JQ, K), 1)
    base = lax.bitwise_xor(row // 4, 1) * 16 + row % 4
    lane = lax.broadcasted_iota(jnp.int32, (16, K), 1)
    small = jnp.zeros((16, K), jnp.int32)
    for sub in range(4):
        for n in range(2):
            small = jnp.where(lane == 4 * sub + n, sides_ref[sub, n], small)
            small = jnp.where(lane == 4 * sub + 2 + n, quarters_ref[sub, n], small)
    small = small.astype(jnp.float32).astype(jnp.bfloat16)
    ordered = jnp.concatenate(
        [centre_ref[:, 1].reshape(HALF, K), centre_ref[:, 0].reshape(HALF, K)], axis=0
    )
    for rho, out in enumerate((keep_ref, mate_ref.at[0], far_ref, mate_ref.at[1])):
        quarter = lax.bitwise_xor(lax.bitwise_xor(grp, rho), 2 * parity)
        pick = jnp.where(col == base + 4 * quarter, 1.0, 0.0).astype(jnp.bfloat16)
        out[:JQ, :] = lax.dot_general(
            pick, ordered, (((1,), (1,)), ((), ())), preferred_element_type=jnp.float32
        ).astype(jnp.bfloat16)
        out[JQ:, :] = small


def split_centres(where, sides, quarters, centre):
    smem = pl.BlockSpec(memory_space=pltpu.SMEM)
    vmem = pl.BlockSpec(memory_space=pltpu.VMEM)
    one = jax.ShapeDtypeStruct((JP, K), jnp.bfloat16)
    two = jax.ShapeDtypeStruct((2, JP, K), jnp.bfloat16)
    return pl.pallas_call(
        split_kernel,
        out_shape=[one, two, one],
        in_specs=[smem, smem, smem, vmem],
        out_specs=[vmem] * 3,
        compiler_params=pltpu.CompilerParams(vmem_limit_bytes=VMEM_LIMIT),
        cost_estimate=LIGHT,
    )(where, sides, quarters, centre.reshape(32, 2, 16, K))


def blend_kernel(first, count, where_ref, params_ref, cross0, cross123, own, side, out_ref, table, sems):
    grp = where_ref[0]
    parity = where_ref[1]
    at = pl.ds(first, count)
    ends = (
        (own, table.at[0:4]),
        (side, table.at[4:8]),
        (cross0.at[at], table.at[8]),
        (cross123.at[:, at], table.at[9:12]),
    )
    copies = [pltpu.make_async_copy(a, b, sems.at[n]) for n, (a, b) in enumerate(ends)]
    for copy in copies:
        copy.start()
    for copy in copies:
        copy.wait()

    @pl.loop(0, 4)
    def _(row):
        i_own = lax.bitwise_xor(lax.bitwise_xor(row, grp), 2)
        plans = []
        for sub in range(4):
            side_row = params_ref[i_own, 4 * sub]
            side_col = params_ref[i_own, 4 * sub + 1]
            a = params_ref[i_own, 4 * sub + 2].astype(jnp.float32) * 0.25
            b = params_ref[i_own, 4 * sub + 3].astype(jnp.float32) * 0.25
            row2 = lax.bitwise_and(row + 2 * side_row - 1, 3)
            base2 = jnp.where(side_col == parity, 0, 4)
            i_row = 8 + lax.bitwise_xor(lax.bitwise_xor(row2, grp), 2)
            i_col = base2 + lax.bitwise_xor(row, grp)
            i_diag = base2 + lax.bitwise_xor(row2, grp)
            terms = ((a * (1.0 - b), i_row), ((1.0 - a) * b, i_col), (a * b, i_diag))
            plans.append(((1.0 - a) * (1.0 - b), terms))

        @pl.loop(0, count // 16, unroll=2)
        def _(step):
            at = pl.ds(pl.multiple_of(step * 16, 16), 16)
            own_part = table[8 + i_own, at, :].astype(jnp.float32)
            for sub, (weight, terms) in enumerate(plans):
                mixed = weight * own_part
                for share, index in terms:
                    mixed = mixed + share * table[index, at, :].astype(jnp.float32)
                out_ref[4 * row + sub, at, :] = mixed.astype(jnp.bfloat16)


def blend_centres(where, params, own, side, cross0, cross123, first, count):
    smem = pl.BlockSpec(memory_space=pltpu.SMEM)
    return pl.pallas_call(
        functools.partial(blend_kernel, first, count),
        out_shape=jax.ShapeDtypeStruct((16, count, K), jnp.bfloat16),
        in_specs=[smem, smem] + [pl.BlockSpec(memory_space=pltpu.HBM)] * 4,
        out_specs=pl.BlockSpec(memory_space=pltpu.VMEM),
        scratch_shapes=[
            pltpu.VMEM((12, count, K), jnp.bfloat16),
            pltpu.SemaphoreType.DMA((4,)),
        ],
        compiler_params=pltpu.CompilerParams(vmem_limit_bytes=VMEM_LIMIT),
        cost_estimate=LIGHT,
    )(where, params, cross0, cross123, own, side)


def sub_block(product, cols, rows):
    lane = lax.broadcasted_iota(jnp.int32, (rows, 128), 1)
    return jnp.where(lane < 64, product[:rows, cols], product[rows:, cols])


def side_by_side(refs, half, row, at):
    return jnp.concatenate(
        [ref[:, half, pl.ds(row, 1), :, at].reshape(HALF, 128) for ref in refs], axis=1
    )


def here_kernel(blend_ref, mine, near, out_ref):
    count = blend_ref.shape[1]

    @pl.loop(0, 4, unroll=4)
    def _(row):
        for pair in range(2):
            at = slice(pair * 128, pair * 128 + 128)
            for two in range(2):
                half = 1 - two
                left = blend_ref[pl.ds(4 * row + 2 * pair, 2), :, half * HALF : half * HALF + HALF]
                product = jnp.dot(
                    left.reshape(2 * count, HALF),
                    side_by_side((mine, near), half, row, at),
                    preferred_element_type=jnp.float32,
                )
                for n in range(2):
                    out_ref[2 * pair + two, n, row] = sub_block(
                        product, slice(n * 128, n * 128 + 128), count
                    )


def apply_here(blend, mine, near):
    vmem = pl.BlockSpec(memory_space=pltpu.VMEM)
    return pl.pallas_call(
        here_kernel,
        out_shape=jax.ShapeDtypeStruct((4, 2, 4, blend.shape[1], 128), jnp.float32),
        in_specs=[vmem] * 3,
        out_specs=vmem,
        compiler_params=pltpu.CompilerParams(vmem_limit_bytes=VMEM_LIMIT),
        cost_estimate=LIGHT,
    )(blend, mine.reshape(32, 2, 4, 16, 256), near.reshape(32, 2, 4, 16, 256))


def apply_kernel(where_ref, blend_a, blend_b, part_a, part_b, far, far_near, out_ref, total):
    quarter = where_ref[2]
    rest = JQ - CUT

    @pl.loop(0, 4, unroll=4)
    def _(row):
        for pair in range(2):
            at = slice(pair * 128, pair * 128 + 128)
            subs = pl.ds(4 * row + 2 * pair, 2)
            for two in range(2):
                lanes = slice(two * HALF, two * HALF + HALF)
                left = jnp.concatenate(
                    [
                        blend_a[subs, :, lanes].reshape(2 * CUT, HALF),
                        blend_b[subs, :, lanes].reshape(2 * rest, HALF),
                    ],
                    axis=0,
                )
                product = jnp.dot(
                    left,
                    side_by_side((far, far_near), two, row, at),
                    preferred_element_type=jnp.float32,
                )
                for n in range(2):
                    cols = slice(n * 128, n * 128 + 128)
                    to = (pair, 2 * two + n)
                    total[(*to, pl.ds(row, CUT, stride=4), slice(None))] = (
                        sub_block(product[: 2 * CUT], cols, CUT) + part_a[2 * pair + two, n, row]
                    )
                    total[(*to, pl.ds(row + 4 * CUT, rest, stride=4), slice(None))] = (
                        sub_block(product[2 * CUT :], cols, rest) + part_b[2 * pair + two, n, row]
                    )

    for rho in range(4):
        level = lax.bitwise_xor(quarter, rho)
        for pair in range(2):
            at = slice(pair * 128, pair * 128 + 128)
            done = total[pair, rho, : 4 * JQ].reshape(32, 2, 16, 128).astype(jnp.bfloat16)
            out_ref[lax.bitwise_xor(level, 2), :, 0, :, at] = done[:, 0]
            out_ref[level, :, 1, :, at] = done[:, 1]


def apply_transforms(where, blend_a, blend_b, part_a, part_b, fields):
    vmem = pl.BlockSpec(memory_space=pltpu.VMEM)
    return pl.pallas_call(
        apply_kernel,
        out_shape=jax.ShapeDtypeStruct((4, 32, 2, 16, 256), jnp.bfloat16),
        in_specs=[pl.BlockSpec(memory_space=pltpu.SMEM)] + [vmem] * 6,
        out_specs=vmem,
        scratch_shapes=[pltpu.VMEM((2, 4, 4 * JQ + 8, 128), jnp.float32)],
        compiler_params=pltpu.CompilerParams(vmem_limit_bytes=VMEM_LIMIT),
        cost_estimate=LIGHT,
    )(where, blend_a, blend_b, part_a, part_b, *(f.reshape(32, 2, 4, 16, 256) for f in fields))


def body(fields, centres, sides, quarters):
    shift = functools.partial(lax.ppermute, axis_name=AX)
    grp = lax.axis_index("grp")
    parity = lax.bitwise_and(lax.axis_index("mem"), 1)
    where = jnp.stack([grp, parity, lax.bitwise_xor(grp, 2 * parity)]).astype(jnp.int32)

    by_col = with_layout_constraint(
        fields[0].transpose(2, 1, 0, 3), Layout(major_to_minor=(0, 1, 2, 3))
    )
    mine = lax.all_to_all(by_col, AX, 0, 0, axis_index_groups=FIELD_GROUPS, tiled=True)

    keep, to_mate, to_far = split_centres(where, sides[0, 0], quarters[0, 0], centres[0, 0])
    mate = shift(to_mate, perm=CORE)
    own23 = shift(jnp.stack([to_far, mate[1]]), perm=PAL)
    cross0 = shift(keep, perm=CROSS)
    own_a = jnp.concatenate([keep[None, :CUT], mate[:1, :CUT], own23[:, :CUT]])
    own_b = jnp.concatenate([keep[None, CUT:JQ], mate[:1, CUT:JQ], own23[:, CUT:JQ]])
    own123 = jnp.concatenate([mate[:1, :JQ], own23[:, :JQ]])
    params = jnp.concatenate([keep[None, JQ, :128], mate[:1, JQ, :128], own23[:, JQ, :128]])
    params = shift(params, perm=CROSS)
    mine, own123, own_a, own_b, cross0, params = lax.optimization_barrier(
        (mine, own123, own_a, own_b, cross0, params)
    )

    far = shift(mine, perm=PAL)
    cross123 = shift(own123, perm=CROSS)
    side_a = shift(own_a, perm=SIDE)
    side_b = shift(shift(shift(own_b, perm=BACK), perm=BACK), perm=BACK_END)
    near = shift(mine, perm=CORE)
    params = params[:, :16].astype(jnp.int32)
    own_far = pltpu.with_memory_space_constraint(own_a, pltpu.HBM)
    blend_a = blend_centres(where, params, own_far, side_a, cross0, cross123, 0, CUT)
    far, blend_a, side_b = lax.optimization_barrier((far, blend_a, side_b))
    far_near = shift(far, perm=CORE)
    part_a = apply_here(blend_a, mine, near)
    blend_b = blend_centres(where, params, own_b, side_b, cross0, cross123, CUT, JQ - CUT)
    part_b = apply_here(blend_b, mine, near)
    result = apply_transforms(where, blend_a, blend_b, part_a, part_b, (far, far_near))

    got = lax.all_to_all(
        result.reshape(MEM * GRP, 16, 256), AX, 0, 0, axis_index_groups=RESULT_GROUP, tiled=True
    )
    return got.reshape(GRP, MEM, 16, 256).transpose(0, 2, 1, 3).reshape(1, 16, 4, MEM, 256)


def solution(mesh):
    return jax.shard_map(
        body,
        mesh=mesh,
        in_specs=(
            P("grp", "mem", None, None, None),
            P("grp", "mem", None, None),
            P("grp", "mem", None, None),
            P("grp", "mem", None, None),
        ),
        out_specs=P("grp", "mem", None, None, None),
        check_vma=False,
    )
```
